128 devices in a mesh: rep: 4 (over z), vocab: 32 (over y, x, core).
Axes of the slice: x: 4, y: 4, z: 4, core: 2. Of those that a mesh axis runs over, the one named last changes fastest.
Arguments:
- queries: bfloat16 [1024, 8192], P(('rep', 'vocab')), may hold values from -160 to 160
- cache_keys: bfloat16 [1024, 256, 1024], P(('rep', 'vocab')), may hold values from -6 to 6
- cache_values: bfloat16 [1024, 256, 1024], P(('rep', 'vocab')), may hold values from -5 to 5
- new_keys: bfloat16 [1024, 1024], P(('rep', 'vocab')), may hold values from -5 to 5
- new_values: bfloat16 [1024, 1024], P(('rep', 'vocab')), may hold values from -5 to 5
- lengths: int32 [1024], P(('rep', 'vocab')), may hold values from 2 to 256, as said below
- residual: bfloat16 [1024, 8192], P(None, ('rep', 'vocab')), may hold values from -140 to 140
- gain: float32 [8192], replicated, may hold values from 0.1 to 1.9
- out_weight: bfloat16 [8192, 8192], P(None, ('rep', 'vocab')), may hold values from -0.25 to 0.25
- head_weight: bfloat16 [8192, 98304], P(None, ('vocab', 'rep')), may hold values from -2.5 to 2.5
- amateur_hidden: bfloat16 [1024, 896], P('rep'), may hold values from -16 to 16
- amateur_head: bfloat16 [896, 98304], P(None, 'vocab'), may hold values from -7 to 7
- thresholds: int32 [1024], replicated, may hold values from 1 to 8
Outputs:
- contrast: float32 [1024, 98304], P(None, ('vocab', 'rep'))
The draws below stay inside these ranges and needn't reach their ends.
Inputs may be any that keep to these rules, and one draw needn't show every extreme that they name: `lengths`: some row's cache is full in every draw.
All inputs are finite; a program needn't handle non-finite values.
Results may differ from the reference program's by a relative error of at most 0.0075.
Values may be sent and summed in bfloat16 or wider, within the bound.
No kernel may reach another device: no remote copies, remote signals or barrier semaphores. Data moves between devices by JAX's collectives and lax.ppermute only.
A program may use at most 128 MiB of HBM per device.

```python
import math
import jax
import jax.numpy as jnp
from jax import lax

D = 8192
QH = 64
KVH = 8
HD = 128
VOCAB = 98304
DA = 896
CACHE = 256
ROWS = 1024


def pair_keys(key):
    key = jax.random.fold_in(key, 303)
    streams = jax.random.split(key, 1)
    first = jnp.clip(jax.random.normal(streams[0], (ROWS, KVH * HD), jnp.float32), -5.0, 5.0)
    return first


def draw_queries(key, part):
    key = jax.random.fold_in(key, 6)
    values = jnp.clip(jax.random.normal(key, (ROWS, QH * HD), jnp.float32), -5.0, 5.0)
    return values.astype(jnp.bfloat16)


def draw_cache_keys(key, part):
    first = pair_keys(key)
    key = jax.random.fold_in(key, 5)
    streams = jax.random.split(key, 1)
    values = jnp.clip(jax.random.normal(streams[0], (ROWS, CACHE, KVH * HD), jnp.float32), -5.0, 5.0)
    positions = jnp.arange(CACHE, dtype=jnp.int32)[None, :, None]
    values = jnp.where(positions == 0, first[:, None, :], values)
    return values.astype(jnp.bfloat16)


def draw_lengths(key, part):
    key = jax.random.fold_in(key, 7)
    streams = jax.random.split(key, 2)
    filled = jax.random.randint(streams[0], (ROWS,), 2, CACHE + 1)
    fullest = jax.random.randint(streams[1], (), 0, ROWS)
    return jnp.where(jnp.arange(ROWS, dtype=jnp.int32) == fullest, CACHE, filled).astype(jnp.int32)


def draw_residual(key, part):
    key = jax.random.fold_in(key, 1)
    streams = jax.random.split(key, 3)
    row_scale = jnp.exp(jax.random.uniform(streams[0], (ROWS, 1), jnp.float32, math.log(0.3), math.log(3.0)))
    col_scale = jnp.exp(jax.random.uniform(streams[1], (1, D), jnp.float32, math.log(0.3), math.log(3.0)))
    col_scale = col_scale * jnp.exp(math.log(3.0) * jnp.arange(D, dtype=jnp.float32)[None, :] / D)
    noise = jnp.clip(jax.random.normal(streams[2], (ROWS, D), jnp.float32), -5.0, 5.0)
    values = noise * row_scale * col_scale
    return values.astype(jnp.bfloat16)


def draw_head_weight(key, part):
    key = jax.random.fold_in(key, 2)
    ramp = 0.7 + 0.9 * jnp.arange(VOCAB, dtype=jnp.float32) / VOCAB
    values = jnp.clip(jax.random.normal(key, (D, VOCAB), jnp.float32), -5.0, 5.0) * (3.0 / math.sqrt(D)) * ramp[None, :]
    return values.astype(jnp.bfloat16)


def draw_amateur_hidden(key, part):
    key = jax.random.fold_in(key, 3)
    streams = jax.random.split(key, 2)
    row_scale = jnp.exp(jax.random.uniform(streams[0], (ROWS, 1), jnp.float32, 0.0, math.log(3.0)))
    noise = jnp.clip(jax.random.normal(streams[1], (ROWS, DA), jnp.float32), -5.0, 5.0)
    values = noise * row_scale
    return values.astype(jnp.bfloat16)


def draw_amateur_head(key, part):
    key = jax.random.fold_in(key, 4)
    ramp = 0.7 + 0.9 * jnp.arange(VOCAB, dtype=jnp.float32) / VOCAB
    values = jnp.clip(jax.random.normal(key, (DA, VOCAB), jnp.float32), -5.0, 5.0) * (3.0 / math.sqrt(DA)) * ramp[None, :]
    return values.astype(jnp.bfloat16)


def plant(array, key, low, high):
    place = [jax.random.randint(jax.random.fold_in(key, axis), (), 0, length) for axis, length in enumerate(array.shape)]
    widest = array.shape.index(max(array.shape))
    neighbour = place[:widest] + [(place[widest] + 1) % array.shape[widest]] + place[widest + 1:]
    return array.at[tuple(place)].set(low).at[tuple(neighbour)].set(high)


def block_scale(key, extent, cuts, least, high):
    loudness, own = 1.0, jax.random.fold_in(key, 6)
    for dim, shards_of in cuts:
        heights = jnp.exp(jax.random.uniform(jax.random.fold_in(own, dim), (shards_of,), jnp.float32, least / len(cuts), high / len(cuts)))
        loudness = loudness * jnp.repeat(heights, extent[dim] // shards_of).reshape([-1 if axis == dim else 1 for axis in range(len(extent))])
    return loudness


def bell_draw(own_key, dims, scale, reach, cuts=(), held_as=jnp.bfloat16):
    array = scale * jax.random.normal(own_key, dims, jnp.float32)
    if cuts:
        array = array * block_scale(own_key, dims, cuts, -0.22, 0.18)
    return jnp.clip(array, -reach, reach).astype(held_as)


def setup_inputs(seed: int = 0) -> dict:
    streams_of = jax.random.split(jax.random.key(seed), 14)
    return {
        "queries": draw_queries(jax.random.fold_in(streams_of[13], 71), 0),
        "cache_keys": draw_cache_keys(jax.random.fold_in(streams_of[13], 71), 0),
        "cache_values": bell_draw(streams_of[2], (ROWS, CACHE, KVH * HD), 1.0, 5.0, ((0, 128),)),
        "new_keys": bell_draw(streams_of[3], (ROWS, KVH * HD), 1.0, 5.0, ((0, 128),)),
        "new_values": bell_draw(streams_of[4], (ROWS, KVH * HD), 1.0, 5.0, ((0, 128),)),
        "lengths": draw_lengths(jax.random.fold_in(streams_of[13], 71), 0),
        "residual": draw_residual(jax.random.fold_in(streams_of[13], 71), 0),
        "gain": jnp.clip(1.0 + 0.18 * jax.random.normal(streams_of[7], (D,), jnp.float32), 0.1, 1.9),
        "out_weight": bell_draw(streams_of[8], (QH * HD, D), (D // 16) ** -0.5, 0.25, ((1, 128),)),
        "head_weight": draw_head_weight(jax.random.fold_in(streams_of[13], 71), 0),
        "amateur_hidden": draw_amateur_hidden(jax.random.fold_in(streams_of[13], 71), 0),
        "amateur_head": draw_amateur_head(jax.random.fold_in(streams_of[13], 71), 0),
        "thresholds": plant(jax.random.randint(streams_of[12], (ROWS,), 1, 9), jax.random.fold_in(streams_of[12], 1), 1, 8).astype(jnp.int32),
    }


EPSILON = 1e-06
LOG_TWO = math.log(2.0)
MASK_FILL = -1e+30

def attend(queries, cache_keys, cache_values, new_keys, new_values, lengths):
    row_count = queries.shape[0]
    groups = QH // KVH
    scaling = HD ** (-0.5)
    query_block = queries.astype(jnp.float32).reshape(row_count, KVH, groups, HD)
    key_block = cache_keys.astype(jnp.float32).reshape(row_count, CACHE, KVH, HD)
    value_block = cache_values.astype(jnp.float32).reshape(row_count, CACHE, KVH, HD)
    scores = jnp.einsum('rkgd,rlkd->rkgl', query_block, key_block) * scaling
    own_score = jnp.einsum('rkgd,rkd->rkg', query_block, new_keys.astype(jnp.float32).reshape(row_count, KVH, HD)) * scaling
    live_mask = (jnp.arange(CACHE, dtype=jnp.int32)[None, :] < lengths[:, None])[:, None, None, :]
    scores = jnp.where(live_mask, scores, MASK_FILL)
    largest = jnp.maximum(lax.optimization_barrier(jnp.max(scores, axis=-1)), own_score)
    weights = jnp.where(live_mask, jnp.exp(scores - largest[..., None]), 0.0)
    own_weight = jnp.exp(own_score - largest)
    totals = lax.optimization_barrier(jnp.sum(weights, axis=-1)) + own_weight
    probabilities = (weights / totals[..., None]).astype(jnp.bfloat16)
    own_probability = (own_weight / totals).astype(jnp.bfloat16)
    mixture = jnp.einsum('rkgl,rlkd->rkgd', probabilities.astype(jnp.float32), value_block)
    mixture = mixture + own_probability.astype(jnp.float32)[..., None] * new_values.astype(jnp.float32).reshape(row_count, KVH, 1, HD)
    return mixture.reshape(row_count, QH * HD).astype(jnp.bfloat16)

def reference(queries, cache_keys, cache_values, new_keys, new_values, lengths, residual, gain, out_weight, head_weight, amateur_hidden, amateur_head, thresholds):
    attention = attend(queries, cache_keys, cache_values, new_keys, new_values, lengths)
    hidden = (residual.astype(jnp.float32) + jnp.dot(attention, out_weight, preferred_element_type=jnp.float32)).astype(jnp.bfloat16)
    widened = hidden.astype(jnp.float32)
    mean_square = lax.optimization_barrier(jnp.mean(widened * widened, axis=1, keepdims=True))
    normed = (widened * lax.rsqrt(mean_square + EPSILON) * gain[None, :]).astype(jnp.bfloat16)
    expert = jnp.dot(normed, head_weight, preferred_element_type=jnp.float32)
    expert_top = lax.optimization_barrier(jnp.max(expert, axis=1, keepdims=True))
    expert_lse = expert_top + jnp.log(lax.optimization_barrier(jnp.sum(jnp.exp(expert - expert_top), axis=1, keepdims=True)))
    rounded = lax.optimization_barrier(jnp.dot(amateur_hidden, amateur_head, preferred_element_type=jnp.float32).astype(jnp.bfloat16))
    amateur = rounded.astype(jnp.float32)
    amateur_top = lax.optimization_barrier(jnp.max(amateur, axis=1, keepdims=True))
    amateur_lse = amateur_top + jnp.log(lax.optimization_barrier(jnp.sum(jnp.exp(amateur - amateur_top), axis=1, keepdims=True)))
    margin = expert - expert_top + thresholds[:, None].astype(jnp.float32) * LOG_TWO
    return expert - expert_lse - (amateur - amateur_lse) + jnp.minimum(margin, 0.0)
```

```python
import functools
import math

import jax
import jax.numpy as jnp
import numpy as np
from jax import lax
from jax.experimental import pallas as pl
from jax.experimental.pallas import tpu as pltpu
from jax.sharding import Mesh
from jax.sharding import PartitionSpec as P

QH = 64
KVH = 8

EPSILON = 1e-06
LOG_TWO = math.log(2.0)
MASK_FILL = -1e30

CHIPS = ("z", "y", "x")
ALL = ("z", "y", "x", "core")
LINE = 128
VMEM = 56 * 1024 * 1024


def attend(queries, cache_keys, cache_values, new_keys, new_values, lengths):
    row_count = queries.shape[0]
    positions = cache_keys.shape[1]
    head_size = queries.shape[1] // QH
    groups = QH // KVH
    scaling = head_size ** (-0.5)
    query_block = queries.reshape(row_count, KVH, groups, head_size)
    key_block = cache_keys.reshape(row_count, positions, KVH, head_size)
    value_block = cache_values.reshape(row_count, positions, KVH, head_size)
    scores = (
        jnp.einsum("rkgd,rlkd->rkgl", query_block, key_block, preferred_element_type=jnp.float32)
        * scaling
    )
    own_score = (
        jnp.einsum(
            "rkgd,rkd->rkg",
            query_block,
            new_keys.reshape(row_count, KVH, head_size),
            preferred_element_type=jnp.float32,
        )
        * scaling
    )
    live_mask = (jnp.arange(positions, dtype=jnp.int32)[None, :] < lengths[:, None])[
        :, None, None, :
    ]
    scores = jnp.where(live_mask, scores, MASK_FILL)
    largest = jnp.maximum(jnp.max(scores, axis=-1), own_score)
    weights = jnp.where(live_mask, jnp.exp(scores - largest[..., None]), 0.0)
    own_weight = jnp.exp(own_score - largest)
    totals = jnp.sum(weights, axis=-1) + own_weight
    probabilities = (weights / totals[..., None]).astype(jnp.bfloat16)
    own_probability = (own_weight / totals).astype(jnp.bfloat16)
    mixture = jnp.einsum(
        "rkgl,rlkd->rkgd", probabilities, value_block, preferred_element_type=jnp.float32
    )
    mixture = mixture + own_probability.astype(jnp.float32)[..., None] * new_values.reshape(
        row_count, KVH, 1, head_size
    ).astype(jnp.float32)
    return mixture.reshape(row_count, QH, head_size).astype(jnp.bfloat16)


def shift(x, axis, step):
    size = lax.axis_size(axis)
    return lax.ppermute(x, axis, [(i, (i + step) % size) for i in range(size)])


def shift_chips(x, offsets):
    sizes = tuple(lax.axis_size(axis) for axis in ALL)
    pairs = []
    for place in np.ndindex(*sizes):
        offset = offsets[place[3]] + (0,)
        target = tuple((a + o) % s for a, o, s in zip(place, offset, sizes))
        pairs.append(
            (int(np.ravel_multi_index(place, sizes)), int(np.ravel_multi_index(target, sizes)))
        )
    return lax.ppermute(x, ALL, pairs)


def quarter_of(z, y, x):
    return (x + 2 * y + z) % 4


def params():
    return pltpu.CompilerParams(vmem_limit_bytes=VMEM)


def laid_along_lanes(largest, totals):
    lane = lax.broadcasted_iota(jnp.int32, (LINE, LINE), 1)
    return jnp.transpose(jnp.where(lane == 0, largest, totals))[:2]


def projection_kernel(left_ref, weight_ref, base_ref, total_ref, sent_ref):
    product = lax.dot_general(
        left_ref[...],
        weight_ref[...],
        (((1,), (1,)), ((), ())),
        preferred_element_type=jnp.float32,
    )
    total_ref[...] = base_ref[...].astype(jnp.float32) + product[:, :LINE]
    for step in range(sent_ref.shape[0]):
        sent_ref[step] = product[:, (step + 1) * LINE : (step + 2) * LINE].astype(jnp.bfloat16)


def project(left, weight, base):
    rows, depth = left.shape
    columns = weight.shape[0]
    return pl.pallas_call(
        projection_kernel,
        out_shape=[
            jax.ShapeDtypeStruct((rows, LINE), jnp.float32),
            jax.ShapeDtypeStruct((columns // LINE - 1, rows, LINE), jnp.bfloat16),
        ],
        compiler_params=params(),
        cost_estimate=pl.CostEstimate(
            flops=2 * rows * depth * columns,
            bytes_accessed=2 * (rows + columns) * depth,
            transcendentals=0,
        ),
        name="projection",
    )(left, weight, base)


def hidden_kernel(places, total_ref, *refs):
    parts, out_ref = refs[:-1], refs[-1]
    total = total_ref[...]
    for part in parts:
        total = total + part[...].astype(jnp.float32)
    hidden = total.astype(jnp.bfloat16)
    for target, quarter in enumerate(places):
        out_ref[target] = hidden[quarter * LINE : quarter * LINE + LINE]


def hidden_copies(total, parts, places):
    return pl.pallas_call(
        functools.partial(hidden_kernel, places),
        out_shape=jax.ShapeDtypeStruct((len(places), LINE, LINE), jnp.bfloat16),
        compiler_params=params(),
        name="hidden",
    )(total, *parts)


def head_kernel(pieces, steps, features, resumed, finished, *refs):
    refs = list(refs)
    gathered = [refs.pop(0) for _ in range(pieces)]
    own_weight, other_weight, gain_ref = [refs.pop(0) for _ in range(3)]
    if resumed:
        own_before, other_before, squares_before = [refs.pop(0) for _ in range(3)]
    own_ref, other_ref, last_ref = [refs.pop(0) for _ in range(3)]
    squares_ref = refs.pop(0) if finished else last_ref
    step = pl.program_id(0)

    @pl.when(step == 0)
    def _():
        own_ref[...] = own_before[...] if resumed else jnp.zeros_like(own_ref)
        other_ref[...] = other_before[...] if resumed else jnp.zeros_like(other_ref)
        squares_ref[...] = squares_before[...] if resumed else jnp.zeros_like(squares_ref)

    rows = []
    for piece in range(pieces):
        blocks = []
        squares = None
        for block in range(gathered[piece].shape[0]):
            wide = gathered[piece][block].astype(jnp.float32)
            squares = wide * wide if squares is None else squares + wide * wide
            blocks.append((wide * gain_ref[block : block + 1]).astype(jnp.bfloat16))
        rows.append(jnp.concatenate(blocks, axis=1))
        squares_ref[piece * LINE : piece * LINE + LINE] += squares
    left = jnp.concatenate(rows, axis=0)
    own_ref[...] += jnp.dot(left, own_weight[...], preferred_element_type=jnp.float32)
    other_ref[...] += jnp.dot(left, other_weight[...], preferred_element_type=jnp.float32)

    if finished:

        @pl.when(step == steps - 1)
        def _():
            for piece in range(pieces):
                tile = slice(piece * LINE, piece * LINE + LINE)
                mean = jnp.sum(squares_ref[tile], axis=1, keepdims=True) / features
                scale = lax.rsqrt(mean + EPSILON)
                own = own_ref[tile] * scale
                other = other_ref[tile] * scale
                own_ref[tile] = own
                other_ref[tile] = other
                largest = jnp.maximum(
                    jnp.max(own, axis=1, keepdims=True), jnp.max(other, axis=1, keepdims=True)
                )
                totals = jnp.sum(jnp.exp(own - largest), axis=1, keepdims=True) + jnp.sum(
                    jnp.exp(other - largest), axis=1, keepdims=True
                )
                last_ref[2 * piece : 2 * piece + 2] = laid_along_lanes(largest, totals)


def head(gathered, own_weight, other_weight, gain, start=0, before=None, finished=True):
    pieces = len(gathered)
    blocks = gathered[0].shape[0]
    features, columns = own_weight.shape
    per = 8
    steps = blocks // per
    first = start // per
    rows = pieces * LINE
    resumed = before is not None
    whole = pl.BlockSpec((rows, columns), lambda i: (0, 0))
    lines = pl.BlockSpec((rows, LINE), lambda i: (0, 0))
    weight = pl.BlockSpec((per * LINE, columns), lambda i: (i + first, 0))
    in_specs = [pl.BlockSpec((per, LINE, LINE), lambda i: (i, 0, 0))] * pieces + [
        weight,
        weight,
        pl.BlockSpec((per, LINE), lambda i: (i + first, 0)),
    ]
    if resumed:
        in_specs += [whole, whole, lines]
    logits = jax.ShapeDtypeStruct((rows, columns), jnp.float32)
    if finished:
        last = jax.ShapeDtypeStruct((2 * pieces, LINE), jnp.float32)
        last_spec = pl.BlockSpec((2 * pieces, LINE), lambda i: (0, 0))
        scratch = [pltpu.VMEM((rows, LINE), jnp.float32)]
    else:
        last = jax.ShapeDtypeStruct((rows, LINE), jnp.float32)
        last_spec = lines
        scratch = []
    return pl.pallas_call(
        functools.partial(head_kernel, pieces, steps, features, resumed, finished),
        grid=(steps,),
        in_specs=in_specs,
        out_specs=[whole, whole, last_spec],
        out_shape=[logits, logits, last],
        scratch_shapes=scratch,
        compiler_params=params(),
        cost_estimate=pl.CostEstimate(
            flops=4 * rows * blocks * LINE * columns,
            bytes_accessed=4 * blocks * LINE * columns,
            transcendentals=0,
        ),
        name="expert_head",
    )(*gathered, own_weight, other_weight, gain, *(before or ()))


def amateur_kernel(place_ref, hidden_ref, weight_ref, logits_ref, stats_ref):
    logits = jnp.dot(
        hidden_ref[...], weight_ref[...], preferred_element_type=jnp.float32
    ).astype(jnp.bfloat16)
    logits_ref[...] = logits
    wide = logits.astype(jnp.float32)
    largest = jnp.max(wide, axis=1, keepdims=True)
    totals = jnp.sum(jnp.exp(wide - largest), axis=1, keepdims=True)
    for plane in range(2):
        picks = range(plane * 8, wide.shape[0], 16)
        stats_ref[0, plane] = laid_along_lanes(
            jnp.concatenate([largest[at : at + 8] for at in picks], axis=0),
            jnp.concatenate([totals[at : at + 8] for at in picks], axis=0),
        )


def amateur_logits(hidden, weight, place, columns):
    rows, width = hidden.shape
    tall = 2 * LINE
    return pl.pallas_call(
        amateur_kernel,
        grid_spec=pltpu.PrefetchScalarGridSpec(
            num_scalar_prefetch=1,
            grid=(rows // tall,),
            in_specs=[
                pl.BlockSpec((tall, width), lambda i, place: (i, 0)),
                pl.BlockSpec((width, columns), lambda i, place: (0, place[0])),
            ],
            out_specs=[
                pl.BlockSpec((tall, columns), lambda i, place: (i, 0)),
                pl.BlockSpec((1, 2, 2, LINE), lambda i, place: (i, 0, 0, 0)),
            ],
        ),
        out_shape=[
            jax.ShapeDtypeStruct((rows, columns), jnp.bfloat16),
            jax.ShapeDtypeStruct((rows // tall, 2, 2, LINE), jnp.float32),
        ],
        compiler_params=params(),
        cost_estimate=pl.CostEstimate(
            flops=2 * rows * width * columns,
            bytes_accessed=2 * (rows * width + width * columns + rows * columns),
            transcendentals=rows * columns,
        ),
        name="amateur_head",
    )(place, hidden, weight)


def merged(parts):
    largest = jnp.max(parts[:, :, 0], axis=0)
    totals = jnp.sum(parts[:, :, 1] * jnp.exp(parts[:, :, 0] - largest[None]), axis=0)
    return largest, totals


def column_of(row):
    return jnp.transpose(jnp.broadcast_to(row, (LINE, LINE)))


def contrast_kernel(
    place_ref,
    own_first,
    own_rest,
    other_first,
    other_rest,
    limit_ref,
    shift_ref,
    amateur_ref,
    out_ref,
    limit_col,
    shift_col,
):
    step = pl.program_id(0)
    tiles = limit_ref.shape[0]
    rows = own_first.shape[0]

    @pl.when(step == 0)
    def _():
        for tile in range(tiles):
            at = slice(tile * LINE, tile * LINE + LINE)
            limit_col[at] = column_of(limit_ref[tile : tile + 1])
            shift_col[at] = column_of(shift_ref[tile : tile + 1])

    def work(own_ref, other_ref):
        first = place_ref[1] == 0
        own, other = own_ref[...], other_ref[...]
        base = lax.rem(place_ref[0] + step // 2, 4) * LINE + lax.rem(step, 2) * rows
        planes = []
        for plane, expert in enumerate(
            (jnp.where(first, own, other), jnp.where(first, other, own))
        ):
            at = pl.ds(pl.multiple_of(base + plane * tiles // 2 * LINE, 8), rows)
            planes.append(
                expert - shift_col[at, :1] + jnp.minimum(expert + limit_col[at, :1], 0.0)
            )
        pieces = []
        for source in range(0, rows, 8):
            pieces += [plane[source : source + 8] for plane in planes]
        out_ref[...] = jnp.concatenate(pieces, axis=0) - amateur_ref[...].astype(jnp.float32)

    @pl.when(step < 2)
    def _():
        work(own_first, other_first)

    @pl.when(step >= 2)
    def _():
        work(own_rest, other_rest)


def contrast(place, own, other, limit, shift, amateur):
    rows, columns = amateur.shape
    half = LINE // 2
    first = pl.BlockSpec((half, columns), lambda i, place: (jnp.minimum(i, 1), 0))
    rest = pl.BlockSpec((half, columns), lambda i, place: (jnp.maximum(i - 2, 0), 0))
    whole = pl.BlockSpec((rows // LINE, LINE), lambda i, place: (0, 0))
    spread = pl.BlockSpec(
        (LINE, columns), lambda i, place: (lax.rem(place[0] + i // 2, 4) * 2 + lax.rem(i, 2), 0)
    )
    return pl.pallas_call(
        contrast_kernel,
        grid_spec=pltpu.PrefetchScalarGridSpec(
            num_scalar_prefetch=1,
            grid=(8,),
            in_specs=[first, rest, first, rest, whole, whole, spread],
            out_specs=spread,
            scratch_shapes=[pltpu.VMEM((rows, LINE), jnp.float32)] * 2,
        ),
        out_shape=jax.ShapeDtypeStruct((rows, columns), jnp.float32),
        compiler_params=params(),
        cost_estimate=pl.CostEstimate(
            flops=6 * rows * columns, bytes_accessed=10 * rows * columns, transcendentals=0
        ),
        name="contrast",
    )(place, own[0], own[1], other[0], other[1], limit, shift, amateur)


def body(
    queries,
    cache_keys,
    cache_values,
    new_keys,
    new_values,
    lengths,
    residual,
    gain,
    out_weight,
    head_weight,
    amateur_hidden,
    amateur_head,
    thresholds,
):
    z, y, x = (lax.axis_index(axis) for axis in CHIPS)
    core = lax.axis_index("core")
    first = core == 0
    sizes = tuple(lax.axis_size(axis) for axis in CHIPS)
    depth, chips = sizes[0], int(np.prod(sizes))
    per, width = queries.shape
    rows = residual.shape[0]
    columns = head_weight.shape[1]
    slab = width // depth
    heads = QH // depth
    quarter = quarter_of(z, y, x)

    other_weight = shift(head_weight, "core", 1)

    turned = out_weight.T
    pieces = []
    for step in range(depth):
        part = lax.dynamic_slice_in_dim(turned, lax.rem(z + step, depth) * slab, slab, 1)
        pieces.append(part if step == 0 else shift(part, "z", step))
    mine = jnp.stack(pieces)
    theirs = shift(mine, "core", 1)
    projection = jnp.stack(
        [jnp.where(first, mine, theirs), jnp.where(first, theirs, mine)], axis=1
    ).reshape(depth * 2 * turned.shape[0], slab)

    planes = residual.T.reshape(-1, chips, 2, per)
    kept = lax.dynamic_index_in_dim(planes, core, 2, False)
    given = shift(lax.dynamic_index_in_dim(planes, 1 - core, 2, False), "core", 1)
    base = jnp.concatenate([jnp.where(first, kept, given), jnp.where(first, given, kept)], axis=0)
    base = base.reshape(-1, chips * per).T

    attention = attend(queries, cache_keys, cache_values, new_keys, new_values, lengths)
    slabs = attention.reshape(per, depth, heads, LINE).transpose(1, 2, 0, 3)
    copies = jnp.broadcast_to(
        slabs.reshape(depth, 1, heads * per, LINE), (depth, chips // depth, heads * per, LINE)
    ).reshape(chips * heads * per, LINE)
    arrived = lax.all_to_all(copies, CHIPS, split_axis=0, concat_axis=0, tiled=True)
    left = arrived.reshape(chips, heads, per, LINE).transpose(0, 2, 1, 3).reshape(chips * per, slab)
    total, sent = project(left, projection, base)
    parts = [shift(sent[step - 1], "z", -step) for step in range(1, depth)]

    places = [quarter_of(*place) for place in np.ndindex(*sizes)]
    quarters = lax.all_to_all(
        hidden_copies(total, parts, places), CHIPS, split_axis=0, concat_axis=0, tiled=True
    )
    moves = (
        ((0, 0, -1), (-1, 0, 0)),
        ((0, -1, 0), (0, 1, 0)),
        ((0, 0, 1), (1, 0, 0)),
    )
    half = chips // 2
    halves = [
        [shift_chips(quarters[at : at + half], move) for move in moves] for at in (0, half)
    ]

    everyone = lax.all_gather(amateur_hidden, "z", axis=0, tiled=True)
    amateur, amateur_stats = amateur_logits(everyone, amateur_head, z.reshape(1), columns)
    by_plane = amateur_stats.transpose(1, 0, 2, 3)
    kept = lax.dynamic_index_in_dim(by_plane, core, 0, False)
    given = shift(lax.dynamic_index_in_dim(by_plane, 1 - core, 0, False), "core", 1)
    amateur_chip = jnp.stack(merged(jnp.stack([kept, given])), axis=1)

    gain_lines = gain.reshape(-1, LINE)
    own_0, other_0, stats_0 = head([quarters], head_weight, other_weight, gain_lines)
    begun = head(halves[0], head_weight, other_weight, gain_lines, finished=False)
    own_1, other_1, stats_1 = head(
        halves[1], head_weight, other_weight, gain_lines, start=half, before=begun
    )
    crossed = [shift(logits, "core", 1) for logits in (other_0, other_1)]

    stats = jnp.concatenate([stats_0, stats_1] * 2).reshape(8, 2, LINE)
    stats = lax.dynamic_slice_in_dim(stats, lax.rem(4 - quarter, 4), 4, 0)
    stats = jnp.concatenate([stats, amateur_chip])
    everywhere = lax.all_to_all(
        jnp.broadcast_to(stats[None], (chips,) + stats.shape).reshape(-1, LINE),
        CHIPS,
        split_axis=0,
        concat_axis=0,
        tiled=True,
    )
    largest, totals = merged(everywhere.reshape((chips,) + stats.shape))
    lse = largest + jnp.log(totals)
    mine = jnp.concatenate([largest[:4], lse[:4] - lse[4:]])
    theirs = shift(mine, "core", 1)
    both = jnp.where(first, jnp.stack([mine, theirs]), jnp.stack([theirs, mine]))
    limit = thresholds.astype(jnp.float32).reshape(chips, 2, per).transpose(1, 0, 2)
    limit = limit.reshape(rows // LINE, LINE) * LOG_TWO - both[:, :4].reshape(rows // LINE, LINE)
    return contrast(
        jnp.stack([quarter, core]),
        (own_0, own_1),
        crossed,
        limit,
        both[:, 4:].reshape(rows // LINE, LINE),
        amateur,
    )


def solution(mesh):
    fine = Mesh(mesh.devices.reshape(4, 4, 4, 2), ALL)
    every = ALL
    by_vocab = ("y", "x", "core")
    in_specs = (
        P(every, None),
        P(every, None, None),
        P(every, None, None),
        P(every, None),
        P(every, None),
        P(every),
        P(None, every),
        P(),
        P(None, every),
        P(None, by_vocab + ("z",)),
        P("z", None),
        P(None, by_vocab),
        P(),
    )
    out_specs = P(None, by_vocab + ("z",))
    return jax.shard_map(body, mesh=fine, in_specs=in_specs, out_specs=out_specs, check_vma=False)
```

```python
import functools
import math

import jax
import jax.numpy as jnp
import numpy as np
from jax import lax
from jax.experimental import pallas as pl
from jax.experimental.pallas import tpu as pltpu
from jax.sharding import Mesh
from jax.sharding import PartitionSpec as P

QH = 64
KVH = 8

EPSILON = 1e-06
LOG_TWO = math.log(2.0)
MASK_FILL = -1e30

CHIPS = ("z", "y", "x")
ALL = ("z", "y", "x", "core")
LINE = 128


def attend(queries, cache_keys, cache_values, new_keys, new_values, lengths):
    row_count = queries.shape[0]
    positions = cache_keys.shape[1]
    head_size = queries.shape[1] // QH
    groups = QH // KVH
    scaling = head_size ** (-0.5)
    query_block = queries.reshape(row_count, KVH, groups, head_size)
    key_block = cache_keys.reshape(row_count, positions, KVH, head_size)
    value_block = cache_values.reshape(row_count, positions, KVH, head_size)
    scores = (
        jnp.einsum("rkgd,rlkd->rkgl", query_block, key_block, preferred_element_type=jnp.float32)
        * scaling
    )
    own_score = (
        jnp.einsum(
            "rkgd,rkd->rkg",
            query_block,
            new_keys.reshape(row_count, KVH, head_size),
            preferred_element_type=jnp.float32,
        )
        * scaling
    )
    live_mask = (jnp.arange(positions, dtype=jnp.int32)[None, :] < lengths[:, None])[
        :, None, None, :
    ]
    scores = jnp.where(live_mask, scores, MASK_FILL)
    largest = jnp.maximum(jnp.max(scores, axis=-1), own_score)
    weights = jnp.where(live_mask, jnp.exp(scores - largest[..., None]), 0.0)
    own_weight = jnp.exp(own_score - largest)
    totals = jnp.sum(weights, axis=-1) + own_weight
    probabilities = (weights / totals[..., None]).astype(jnp.bfloat16)
    own_probability = (own_weight / totals).astype(jnp.bfloat16)
    mixture = jnp.einsum(
        "rkgl,rlkd->rkgd", probabilities, value_block, preferred_element_type=jnp.float32
    )
    mixture = mixture + own_probability.astype(jnp.float32)[..., None] * new_values.reshape(
        row_count, KVH, 1, head_size
    ).astype(jnp.float32)
    return mixture.reshape(row_count, QH, head_size).astype(jnp.bfloat16)


def shift(x, axis, step):
    size = lax.axis_size(axis)
    return lax.ppermute(x, axis, [(i, (i + step) % size) for i in range(size)])


def shift_chips(x, offsets):
    sizes = tuple(lax.axis_size(axis) for axis in ALL)
    pairs = []
    for place in np.ndindex(*sizes):
        offset = offsets[place[3]] + (0,)
        target = tuple((a + o) % s for a, o, s in zip(place, offset, sizes))
        pairs.append(
            (int(np.ravel_multi_index(place, sizes)), int(np.ravel_multi_index(target, sizes)))
        )
    return lax.ppermute(x, ALL, pairs)


def quarter_of(z, y, x):
    return (x + 2 * y + z) % 4


def params(mebibytes):
    return pltpu.CompilerParams(vmem_limit_bytes=mebibytes * 1024 * 1024)


def laid_along_lanes(largest, totals):
    lane = lax.broadcasted_iota(jnp.int32, (LINE, LINE), 1)
    return jnp.transpose(jnp.where(lane == 0, largest, totals))[:2]


def projection_kernel(left_ref, weight_ref, base_ref, total_ref, *sent):
    product = lax.dot_general(
        left_ref[...],
        weight_ref[...],
        (((1,), (1,)), ((), ())),
        preferred_element_type=jnp.float32,
    )
    total_ref[...] = base_ref[...].astype(jnp.float32) + product[:, :LINE]
    for step, sent_ref in enumerate(sent, 1):
        sent_ref[...] = product[:, step * LINE : (step + 1) * LINE].astype(jnp.bfloat16)


def project(left, weight, base):
    rows, depth = left.shape
    columns = weight.shape[0]
    return pl.pallas_call(
        projection_kernel,
        out_shape=[jax.ShapeDtypeStruct((rows, LINE), jnp.float32)]
        + [jax.ShapeDtypeStruct((rows, LINE), jnp.bfloat16)] * (columns // LINE - 1),
        compiler_params=params(16),
        cost_estimate=pl.CostEstimate(
            flops=2 * rows * depth * columns,
            bytes_accessed=2 * (rows + columns) * depth,
            transcendentals=0,
        ),
        name="projection",
    )(left, weight, base)


def hidden_kernel(turns, total_ref, *refs):
    parts, out_ref, hidden_ref, sem = refs[:-3], refs[-3], refs[-2], refs[-1]
    total = total_ref[...]
    for part in parts:
        total = total + part[...].astype(jnp.float32)
    hidden = total.astype(jnp.bfloat16)
    rows = hidden.shape[0]
    hidden_ref[:rows] = hidden
    hidden_ref[rows:] = hidden
    copies = [
        pltpu.make_async_copy(
            hidden_ref.at[pl.ds(turn * LINE, rows)], out_ref.at[line], sem.at[line]
        )
        for line, turn in enumerate(turns)
    ]
    for copy in copies:
        copy.start()
    for copy in copies:
        copy.wait()


def hidden_copies(total, parts, turns):
    rows = total.shape[0]
    return pl.pallas_call(
        functools.partial(hidden_kernel, turns),
        out_specs=pl.BlockSpec(memory_space=pl.ANY),
        out_shape=jax.ShapeDtypeStruct((len(turns), rows, LINE), jnp.bfloat16),
        scratch_shapes=[
            pltpu.VMEM((2 * rows, LINE), jnp.bfloat16),
            pltpu.SemaphoreType.DMA((len(turns),)),
        ],
        compiler_params=params(60),
        name="hidden",
    )(total, *parts)


def head_kernel(pieces, steps, features, resumed, finished, *refs):
    refs = list(refs)
    gathered = [refs.pop(0) for _ in range(pieces)]
    own_weight, other_weight, gain_ref = [refs.pop(0) for _ in range(3)]
    if resumed:
        own_before, other_before, squares_before = [refs.pop(0) for _ in range(3)]
    own_ref, other_ref, last_ref = [refs.pop(0) for _ in range(3)]
    squares_ref = refs.pop(0) if finished else last_ref
    step = pl.program_id(0)

    @pl.when(step == 0)
    def _():
        own_ref[...] = own_before[...] if resumed else jnp.zeros_like(own_ref)
        other_ref[...] = other_before[...] if resumed else jnp.zeros_like(other_ref)
        squares_ref[...] = squares_before[...] if resumed else jnp.zeros_like(squares_ref)

    rows = []
    for piece in range(pieces):
        blocks = []
        squares = None
        for block in range(gathered[piece].shape[0]):
            wide = gathered[piece][block].astype(jnp.float32)
            squares = wide * wide if squares is None else squares + wide * wide
            blocks.append((wide * gain_ref[block : block + 1]).astype(jnp.bfloat16))
        rows.append(jnp.concatenate(blocks, axis=1))
        squares_ref[piece * LINE : piece * LINE + LINE] += squares
    left = jnp.concatenate(rows, axis=0)
    own_ref[...] += jnp.dot(left, own_weight[...], preferred_element_type=jnp.float32)
    other_ref[...] += jnp.dot(left, other_weight[...], preferred_element_type=jnp.float32)

    if finished:

        @pl.when(step == steps - 1)
        def _():
            for piece in range(pieces):
                tile = slice(piece * LINE, piece * LINE + LINE)
                mean = jnp.sum(squares_ref[tile], axis=1, keepdims=True) / features
                scale = lax.rsqrt(mean + EPSILON)
                own = own_ref[tile] * scale
                other = other_ref[tile] * scale
                own_ref[tile] = own
                other_ref[tile] = other
                largest = jnp.maximum(
                    jnp.max(own, axis=1, keepdims=True), jnp.max(other, axis=1, keepdims=True)
                )
                totals = jnp.sum(jnp.exp(own - largest), axis=1, keepdims=True) + jnp.sum(
                    jnp.exp(other - largest), axis=1, keepdims=True
                )
                last_ref[2 * piece : 2 * piece + 2] = laid_along_lanes(largest, totals)


def head(gathered, own_weight, other_weight, gain, start=0, before=None, finished=True):
    pieces = len(gathered)
    blocks = gathered[0].shape[0]
    features, columns = own_weight.shape
    per = 8
    steps = blocks // per
    first = start // per
    rows = pieces * LINE
    resumed = before is not None
    whole = pl.BlockSpec((rows, columns), lambda i: (0, 0))
    lines = pl.BlockSpec((rows, LINE), lambda i: (0, 0))
    weight = pl.BlockSpec((per * LINE, columns), lambda i: (i + first, 0))
    in_specs = [pl.BlockSpec((per, LINE, LINE), lambda i: (i, 0, 0))] * pieces + [
        weight,
        weight,
        pl.BlockSpec((per, LINE), lambda i: (i + first, 0)),
    ]
    if resumed:
        in_specs += [whole, whole, lines]
    logits = jax.ShapeDtypeStruct((rows, columns), jnp.float32)
    if finished:
        last = jax.ShapeDtypeStruct((2 * pieces, LINE), jnp.float32)
        last_spec = pl.BlockSpec((2 * pieces, LINE), lambda i: (0, 0))
        scratch = [pltpu.VMEM((rows, LINE), jnp.float32)]
    else:
        last = jax.ShapeDtypeStruct((rows, LINE), jnp.float32)
        last_spec = lines
        scratch = []
    return pl.pallas_call(
        functools.partial(head_kernel, pieces, steps, features, resumed, finished),
        grid=(steps,),
        in_specs=in_specs,
        out_specs=[whole, whole, last_spec],
        out_shape=[logits, logits, last],
        scratch_shapes=scratch,
        compiler_params=params(26),
        cost_estimate=pl.CostEstimate(
            flops=4 * rows * blocks * LINE * columns,
            bytes_accessed=4 * blocks * LINE * columns,
            transcendentals=0,
        ),
        name="expert_head",
    )(*gathered, own_weight, other_weight, gain, *(before or ()))


def amateur_kernel(place_ref, hidden_ref, weight_ref, logits_ref, stats_ref):
    logits = jnp.dot(
        hidden_ref[...], weight_ref[...], preferred_element_type=jnp.float32
    ).astype(jnp.bfloat16)
    logits_ref[...] = logits
    wide = logits.astype(jnp.float32)
    largest = jnp.max(wide, axis=1, keepdims=True)
    totals = jnp.sum(jnp.exp(wide - largest), axis=1, keepdims=True)
    for plane in range(2):
        picks = range(plane * 8, wide.shape[0], 16)
        stats_ref[0, plane] = laid_along_lanes(
            jnp.concatenate([largest[at : at + 8] for at in picks], axis=0),
            jnp.concatenate([totals[at : at + 8] for at in picks], axis=0),
        )


def amateur_logits(hidden, weight, place, columns):
    rows, width = hidden.shape
    tall = 2 * LINE
    return pl.pallas_call(
        amateur_kernel,
        grid_spec=pltpu.PrefetchScalarGridSpec(
            num_scalar_prefetch=1,
            grid=(rows // tall,),
            in_specs=[
                pl.BlockSpec((tall, width), lambda i, place: (i, 0)),
                pl.BlockSpec((width, columns), lambda i, place: (0, place[0])),
            ],
            out_specs=[
                pl.BlockSpec((tall, columns), lambda i, place: (i, 0)),
                pl.BlockSpec((1, 2, 2, LINE), lambda i, place: (i, 0, 0, 0)),
            ],
        ),
        out_shape=[
            jax.ShapeDtypeStruct((rows, columns), jnp.bfloat16),
            jax.ShapeDtypeStruct((rows // tall, 2, 2, LINE), jnp.float32),
        ],
        compiler_params=params(16),
        cost_estimate=pl.CostEstimate(
            flops=2 * rows * width * columns,
            bytes_accessed=2 * (rows * width + width * columns + rows * columns),
            transcendentals=rows * columns,
        ),
        name="amateur_head",
    )(place, hidden, weight)


def merged(parts):
    largest = jnp.max(parts[:, :, 0], axis=0)
    totals = jnp.sum(parts[:, :, 1] * jnp.exp(parts[:, :, 0] - largest[None]), axis=0)
    return largest, totals


def spread_kernel(
    place_ref, first_ref, rest_ref, amateur_ref, out_ref, stats_ref, group_ref, sem
):
    quarters = amateur_ref.shape[0] // 2
    for piece in range(quarters):
        at = pl.ds(2 * lax.rem(place_ref[0] + piece, quarters), 2)
        stats_ref[at] = first_ref[...] if piece == 0 else rest_ref[2 * piece - 2 : 2 * piece]
    stats_ref[2 * quarters :] = amateur_ref[...]
    for target in range(group_ref.shape[0]):
        group_ref[target] = stats_ref[...]
    many = group_ref.shape[0]
    copies = [
        pltpu.make_async_copy(group_ref, out_ref.at[pl.ds(at, many)], sem.at[at // many])
        for at in range(0, out_ref.shape[0], many)
    ]
    for copy in copies:
        copy.start()
    for copy in copies:
        copy.wait()


def spread(place, first, rest, amateur, targets):
    rows = 2 * amateur.shape[0]
    vmem = pl.BlockSpec(memory_space=pltpu.VMEM)
    return pl.pallas_call(
        spread_kernel,
        in_specs=[pl.BlockSpec(memory_space=pltpu.SMEM)] + [vmem] * 3,
        out_specs=pl.BlockSpec(memory_space=pl.ANY),
        out_shape=jax.ShapeDtypeStruct((targets, rows, LINE), jnp.float32),
        scratch_shapes=[
            pltpu.VMEM((rows, LINE), jnp.float32),
            pltpu.VMEM((8, rows, LINE), jnp.float32),
            pltpu.SemaphoreType.DMA((targets // 8,)),
        ],
        compiler_params=params(60),
        name="spread_stats",
    )(place, first, rest, amateur)


def merge_kernel(parts_ref, out_ref):
    parts = parts_ref[...]
    largest = jnp.max(parts, axis=0)
    quarters = out_ref.shape[0] // 2
    tops, sums = [], []
    for tile in range(2 * quarters):
        top = largest[2 * tile : 2 * tile + 1]
        scales = jnp.exp(parts[:, 2 * tile] - top)
        tops.append(top)
        sums.append(
            top + jnp.log(jnp.sum(parts[:, 2 * tile + 1] * scales, axis=0, keepdims=True))
        )
    shifts = [sums[tile] - sums[quarters + tile] for tile in range(quarters)]
    out_ref[...] = jnp.concatenate(tops[:quarters] + shifts, axis=0)


def merge(parts):
    return pl.pallas_call(
        merge_kernel,
        out_shape=jax.ShapeDtypeStruct((parts.shape[1] // 2, LINE), jnp.float32),
        compiler_params=params(8),
        name="merge_stats",
    )(parts)


def column_of(row):
    return jnp.transpose(jnp.broadcast_to(row, (LINE, LINE)))


def contrast_kernel(
    place_ref,
    mine_ref,
    theirs_ref,
    limit_ref,
    own_first_in,
    own_rest_in,
    other_first_in,
    other_rest_in,
    amateur_in,
    out_ref,
    own_first,
    own_rest,
    other_first,
    other_rest,
    amateur_ref,
    result_ref,
    sem,
    sem_in,
):
    arrivals = [
        pltpu.make_async_copy(source, target, sem_in.at[i])
        for i, (source, target) in enumerate(
            (
                (own_first_in, own_first),
                (other_first_in, other_first),
                (amateur_in, amateur_ref),
                (own_rest_in, own_rest),
                (other_rest_in, other_rest),
            )
        )
    ]
    for copy in arrivals:
        copy.start()
    core = place_ref[1]
    first = core == 0
    quarters = limit_ref.shape[0] // 2
    tall = 2 * LINE
    step_rows = 32
    copies = []
    for piece in range(quarters):
        quarter = lax.rem(place_ref[0] + piece, quarters)
        start = pl.multiple_of(quarter * tall, tall)
        sides = []
        for stats, plane in ((mine_ref, core), (theirs_ref, 1 - core)):
            top = stats[pl.ds(quarter, 1)]
            limit = limit_ref[pl.ds(plane * quarters + quarter, 1)]
            sides.append(
                (column_of(limit - top), column_of(stats[pl.ds(quarters + quarter, 1)]))
            )
        for copy in (arrivals[:3], arrivals[3:], (), ())[piece]:
            copy.wait()
        experts = (own_first, other_first) if piece == 0 else (own_rest, other_rest)
        offset = 0 if piece == 0 else (piece - 1) * LINE
        for at in range(0, LINE, step_rows):
            rows = slice(at, at + step_rows)
            own, other = (
                expert - shift[rows, :1] + jnp.minimum(expert + limit[rows, :1], 0.0)
                for expert, (limit, shift) in zip(
                    (ref[offset + at : offset + at + step_rows] for ref in experts), sides
                )
            )
            planes = (jnp.where(first, own, other), jnp.where(first, other, own))
            mixed = jnp.concatenate(
                [plane[i : i + 8] for i in range(0, step_rows, 8) for plane in planes], axis=0
            )
            amateur = amateur_ref[pl.ds(pl.multiple_of(start + 2 * at, 2 * step_rows), 2 * step_rows)]
            result_ref[piece, 2 * at : 2 * at + 2 * step_rows] = mixed - amateur.astype(jnp.float32)
        copy = pltpu.make_async_copy(
            result_ref.at[piece], out_ref.at[pl.ds(start, tall)], sem.at[piece]
        )
        copy.start()
        copies.append(copy)
    for copy in copies:
        copy.wait()


def contrast(place, mine, theirs, limit, own, other, amateur):
    rows, columns = amateur.shape
    vmem = pl.BlockSpec(memory_space=pltpu.VMEM)
    return pl.pallas_call(
        contrast_kernel,
        in_specs=[pl.BlockSpec(memory_space=pltpu.SMEM)]
        + [vmem] * 3
        + [pl.BlockSpec(memory_space=pl.ANY)] * 5,
        out_specs=pl.BlockSpec(memory_space=pl.ANY),
        out_shape=jax.ShapeDtypeStruct((rows, columns), jnp.float32),
        scratch_shapes=[pltpu.VMEM(a.shape, a.dtype) for a in (*own, *other, amateur)]
        + [
            pltpu.VMEM((rows // (2 * LINE), 2 * LINE, columns), jnp.float32),
            pltpu.SemaphoreType.DMA((rows // (2 * LINE),)),
            pltpu.SemaphoreType.DMA((5,)),
        ],
        compiler_params=params(60),
        cost_estimate=pl.CostEstimate(
            flops=6 * rows * columns, bytes_accessed=10 * rows * columns, transcendentals=0
        ),
        name="contrast",
    )(place, mine, theirs, limit, own[0], own[1], other[0], other[1], amateur)


def body(
    queries,
    cache_keys,
    cache_values,
    new_keys,
    new_values,
    lengths,
    residual,
    gain,
    out_weight,
    head_weight,
    amateur_hidden,
    amateur_head,
    thresholds,
):
    z, y, x = (lax.axis_index(axis) for axis in CHIPS)
    core = lax.axis_index("core")
    first = core == 0
    sizes = tuple(lax.axis_size(axis) for axis in CHIPS)
    depth, chips = sizes[0], int(np.prod(sizes))
    per, width = queries.shape
    rows = residual.shape[0]
    columns = head_weight.shape[1]
    slab = width // depth
    heads = QH // depth
    quarter = quarter_of(z, y, x)

    attention = attend(queries, cache_keys, cache_values, new_keys, new_values, lengths)
    slabs = attention.reshape(per, depth, heads, LINE).transpose(1, 2, 0, 3)
    copies = jnp.broadcast_to(
        slabs.reshape(depth, 1, heads * per, LINE), (depth, chips // depth, heads * per, LINE)
    ).reshape(chips * heads * per, LINE)
    copies, residual = lax.optimization_barrier((copies, residual))
    everyone = lax.all_gather(amateur_hidden, "z", axis=0, tiled=True)
    arrived = lax.all_to_all(copies, CHIPS, split_axis=0, concat_axis=0, tiled=True)

    other_weight = shift(head_weight, "core", 1)

    turned = out_weight.T
    pieces = []
    for step in range(depth):
        part = lax.dynamic_slice_in_dim(turned, lax.rem(z + step, depth) * slab, slab, 1)
        pieces.append(part if step == 0 else shift(part, "z", step))
    mine = jnp.stack(pieces)
    theirs = shift(mine, "core", 1)
    projection = jnp.stack(
        [jnp.where(first, mine, theirs), jnp.where(first, theirs, mine)], axis=1
    ).reshape(depth * 2 * turned.shape[0], slab)

    planes = residual.T.reshape(-1, chips, 2, per)
    kept = lax.dynamic_index_in_dim(planes, core, 2, False)
    given = shift(lax.dynamic_index_in_dim(planes, 1 - core, 2, False), "core", 1)
    base = jnp.concatenate([jnp.where(first, kept, given), jnp.where(first, given, kept)], axis=0)
    base = base.reshape(-1, chips * per).T

    left = arrived.reshape(chips, heads, per, LINE).transpose(0, 2, 1, 3).reshape(chips * per, slab)
    total, *sent = project(left, projection, base)
    parts = [shift(part, "z", -step) for step, part in enumerate(sent, 1)]
    total, everyone = lax.optimization_barrier((total, everyone))

    turns = [quarter_of(*place, 0) for place in np.ndindex(*sizes[:2])]
    copies = hidden_copies(total, parts, turns).reshape(chips, LINE, LINE)
    quarters = lax.all_to_all(copies, CHIPS, split_axis=0, concat_axis=0, tiled=True)
    amateur, amateur_stats = amateur_logits(everyone, amateur_head, z.reshape(1), columns)
    by_plane = amateur_stats.transpose(1, 0, 2, 3)
    kept = lax.dynamic_index_in_dim(by_plane, core, 0, False)
    given = shift(lax.dynamic_index_in_dim(by_plane, 1 - core, 0, False), "core", 1)
    amateur_chip = jnp.stack(merged(jnp.stack([kept, given])), axis=1)

    limit = thresholds.astype(jnp.float32).reshape(chips, 2, per).transpose(1, 0, 2)
    limit = limit.reshape(rows // LINE, LINE) * LOG_TWO
    place = jnp.stack([quarter, core])
    quarters, amateur, amateur_chip, limit, place = lax.optimization_barrier(
        (quarters, amateur, amateur_chip, limit, place)
    )
    moves = (
        ((0, 0, -1), (-1, 0, 0)),
        ((0, -1, 0), (0, 1, 0)),
        ((0, 0, 1), (1, 0, 0)),
    )
    half = chips * 5 // 8

    gain_lines = gain.reshape(-1, LINE)
    halves = [[shift_chips(quarters[:half], move) for move in moves]]
    halves.append([shift_chips(quarters[half:], move) for move in moves[:2]])
    own_0, other_0, stats_0 = head([quarters], head_weight, other_weight, gain_lines)
    later, own_0 = lax.optimization_barrier((quarters[half:], own_0))
    halves[1].append(shift_chips(later, moves[2]))
    begun = head(halves[0], head_weight, other_weight, gain_lines, finished=False)
    own_1, other_1, stats_1 = head(
        halves[1], head_weight, other_weight, gain_lines, start=half, before=begun
    )
    crossed = [shift(logits, "core", 1) for logits in (other_0, other_1)]

    copies = spread(place, stats_0, stats_1, amateur_chip.reshape(-1, LINE), chips)
    mine = merge(lax.all_to_all(copies, CHIPS, split_axis=0, concat_axis=0, tiled=True))
    theirs = shift(mine, "core", 1)
    return contrast(place, mine, theirs, limit, (own_0, own_1), crossed, amateur)


def solution(mesh):
    fine = Mesh(mesh.devices.reshape(4, 4, 4, 2), ALL)
    every = ALL
    by_vocab = ("y", "x", "core")
    in_specs = (
        P(every, None),
        P(every, None, None),
        P(every, None, None),
        P(every, None),
        P(every, None),
        P(every),
        P(None, every),
        P(),
        P(None, every),
        P(None, by_vocab + ("z",)),
        P("z", None),
        P(None, by_vocab),
        P(),
    )
    out_specs = P(None, by_vocab + ("z",))
    return jax.shard_map(body, mesh=fine, in_specs=in_specs, out_specs=out_specs, check_vma=False)
```

```python
import functools
import math

import jax
import jax.numpy as jnp
import numpy as np
from jax import lax
from jax.experimental import pallas as pl
from jax.experimental.pallas import tpu as pltpu
from jax.sharding import Mesh
from jax.sharding import PartitionSpec as P

QH = 64
KVH = 8

EPSILON = 1e-06
LOG_TWO = math.log(2.0)
MASK_FILL = -1e30

CHIPS = ("z", "y", "x")
ALL = ("z", "y", "x", "core")
LINE = 128


def attend(queries, cache_keys, cache_values, new_keys, new_values, lengths):
    row_count = queries.shape[0]
    positions = cache_keys.shape[1]
    head_size = queries.shape[1] // QH
    groups = QH // KVH
    scaling = head_size ** (-0.5)
    query_block = queries.reshape(row_count, KVH, groups, head_size)
    key_block = cache_keys.reshape(row_count, positions, KVH, head_size)
    value_block = cache_values.reshape(row_count, positions, KVH, head_size)
    scores = (
        jnp.einsum("rkgd,rlkd->rkgl", query_block, key_block, preferred_element_type=jnp.float32)
        * scaling
    )
    own_score = (
        jnp.einsum(
            "rkgd,rkd->rkg",
            query_block,
            new_keys.reshape(row_count, KVH, head_size),
            preferred_element_type=jnp.float32,
        )
        * scaling
    )
    live_mask = (jnp.arange(positions, dtype=jnp.int32)[None, :] < lengths[:, None])[
        :, None, None, :
    ]
    scores = jnp.where(live_mask, scores, MASK_FILL)
    largest = jnp.maximum(jnp.max(scores, axis=-1), own_score)
    weights = jnp.where(live_mask, jnp.exp(scores - largest[..., None]), 0.0)
    own_weight = jnp.exp(own_score - largest)
    totals = jnp.sum(weights, axis=-1) + own_weight
    probabilities = (weights / totals[..., None]).astype(jnp.bfloat16)
    own_probability = (own_weight / totals).astype(jnp.bfloat16)
    mixture = jnp.einsum(
        "rkgl,rlkd->rkgd", probabilities, value_block, preferred_element_type=jnp.float32
    )
    mixture = mixture + own_probability.astype(jnp.float32)[..., None] * new_values.reshape(
        row_count, KVH, 1, head_size
    ).astype(jnp.float32)
    return mixture.reshape(row_count, QH, head_size).astype(jnp.bfloat16)


def shift(x, axis, step):
    size = lax.axis_size(axis)
    return lax.ppermute(x, axis, [(i, (i + step) % size) for i in range(size)])


def shift_chips(x, offsets):
    sizes = tuple(lax.axis_size(axis) for axis in ALL)
    pairs = []
    for place in np.ndindex(*sizes):
        offset = offsets[place[3]] + (0,)
        target = tuple((a + o) % s for a, o, s in zip(place, offset, sizes))
        pairs.append(
            (int(np.ravel_multi_index(place, sizes)), int(np.ravel_multi_index(target, sizes)))
        )
    return lax.ppermute(x, ALL, pairs)


def quarter_of(z, y, x):
    return (x + 2 * y + z) % 4


def params(mebibytes):
    return pltpu.CompilerParams(vmem_limit_bytes=mebibytes * 1024 * 1024)


def laid_along_lanes(largest, totals):
    lane = lax.broadcasted_iota(jnp.int32, (LINE, LINE), 1)
    return jnp.transpose(jnp.where(lane == 0, largest, totals))[:2]


def projection_kernel(left_ref, weight_ref, base_ref, total_ref, *sent):
    product = lax.dot_general(
        left_ref[...],
        weight_ref[...],
        (((1,), (1,)), ((), ())),
        preferred_element_type=jnp.float32,
    )
    total_ref[...] = base_ref[...].astype(jnp.float32) + product[:, :LINE]
    for step, sent_ref in enumerate(sent, 1):
        sent_ref[...] = product[:, step * LINE : (step + 1) * LINE].astype(jnp.bfloat16)


def project(left, weight, base):
    rows, depth = left.shape
    columns = weight.shape[0]
    return pl.pallas_call(
        projection_kernel,
        out_shape=[jax.ShapeDtypeStruct((rows, LINE), jnp.float32)]
        + [jax.ShapeDtypeStruct((rows, LINE), jnp.bfloat16)] * (columns // LINE - 1),
        compiler_params=params(16),
        cost_estimate=pl.CostEstimate(
            flops=2 * rows * depth * columns,
            bytes_accessed=2 * (rows + columns) * depth,
            transcendentals=0,
        ),
        name="projection",
    )(left, weight, base)


def hidden_kernel(turns, total_ref, *refs):
    parts, out_ref, hidden_ref, sem = refs[:-3], refs[-3], refs[-2], refs[-1]
    total = total_ref[...]
    for part in parts:
        total = total + part[...].astype(jnp.float32)
    hidden = total.astype(jnp.bfloat16)
    rows = hidden.shape[0]
    hidden_ref[:rows] = hidden
    hidden_ref[rows:] = hidden
    copies = [
        pltpu.make_async_copy(
            hidden_ref.at[pl.ds(turn * LINE, rows)], out_ref.at[line], sem.at[line]
        )
        for line, turn in enumerate(turns)
    ]
    for copy in copies:
        copy.start()
    for copy in copies:
        copy.wait()


def hidden_copies(total, parts, turns):
    rows = total.shape[0]
    return pl.pallas_call(
        functools.partial(hidden_kernel, turns),
        out_specs=pl.BlockSpec(memory_space=pltpu.HBM),
        out_shape=pltpu.HBM((len(turns), rows, LINE), jnp.bfloat16),
        scratch_shapes=[
            pltpu.VMEM((2 * rows, LINE), jnp.bfloat16),
            pltpu.SemaphoreType.DMA((len(turns),)),
        ],
        compiler_params=params(8),
        name="hidden",
    )(total, *parts)


def head_kernel(pieces, steps, features, resumed, finished, *refs):
    refs = list(refs)
    gathered = [refs.pop(0) for _ in range(pieces)]
    own_weight, other_weight, gain_ref = [refs.pop(0) for _ in range(3)]
    if resumed:
        own_before, other_before, squares_before = [refs.pop(0) for _ in range(3)]
    own_ref, other_ref, last_ref = [refs.pop(0) for _ in range(3)]
    squares_ref = refs.pop(0) if finished else last_ref
    step = pl.program_id(0)

    @pl.when(step == 0)
    def _():
        own_ref[...] = own_before[...] if resumed else jnp.zeros_like(own_ref)
        other_ref[...] = other_before[...] if resumed else jnp.zeros_like(other_ref)
        squares_ref[...] = squares_before[...] if resumed else jnp.zeros_like(squares_ref)

    rows = []
    for piece in range(pieces):
        blocks = []
        squares = None
        for block in range(gathered[piece].shape[0]):
            wide = gathered[piece][block].astype(jnp.float32)
            squares = wide * wide if squares is None else squares + wide * wide
            blocks.append((wide * gain_ref[block : block + 1]).astype(jnp.bfloat16))
        rows.append(jnp.concatenate(blocks, axis=1))
        squares_ref[piece * LINE : piece * LINE + LINE] += squares
    left = jnp.concatenate(rows, axis=0)
    own_ref[...] += jnp.dot(left, own_weight[...], preferred_element_type=jnp.float32)
    other_ref[...] += jnp.dot(left, other_weight[...], preferred_element_type=jnp.float32)

    if finished:

        @pl.when(step == steps - 1)
        def _():
            for piece in range(pieces):
                tile = slice(piece * LINE, piece * LINE + LINE)
                mean = jnp.sum(squares_ref[tile], axis=1, keepdims=True) / features
                scale = lax.rsqrt(mean + EPSILON)
                own = own_ref[tile] * scale
                other = other_ref[tile] * scale
                own_ref[tile] = own
                other_ref[tile] = other
                largest = jnp.maximum(
                    jnp.max(own, axis=1, keepdims=True), jnp.max(other, axis=1, keepdims=True)
                )
                totals = jnp.sum(jnp.exp(own - largest), axis=1, keepdims=True) + jnp.sum(
                    jnp.exp(other - largest), axis=1, keepdims=True
                )
                last_ref[2 * piece : 2 * piece + 2] = laid_along_lanes(largest, totals)


def head(gathered, own_weight, other_weight, gain, start=0, before=None, finished=True):
    pieces = len(gathered)
    blocks = gathered[0].shape[0]
    features, columns = own_weight.shape
    per = 8
    steps = blocks // per
    first = start // per
    rows = pieces * LINE
    resumed = before is not None
    whole = pl.BlockSpec((rows, columns), lambda i: (0, 0))
    lines = pl.BlockSpec((rows, LINE), lambda i: (0, 0))
    weight = pl.BlockSpec((per * LINE, columns), lambda i: (i + first, 0))
    in_specs = [pl.BlockSpec((per, LINE, LINE), lambda i: (i, 0, 0))] * pieces + [
        weight,
        weight,
        pl.BlockSpec((per, LINE), lambda i: (i + first, 0)),
    ]
    if resumed:
        in_specs += [whole, whole, lines]
    logits = jax.ShapeDtypeStruct((rows, columns), jnp.float32)
    if finished:
        logits = pltpu.HBM(logits.shape, logits.dtype)
        last = jax.ShapeDtypeStruct((2 * pieces, LINE), jnp.float32)
        last_spec = pl.BlockSpec((2 * pieces, LINE), lambda i: (0, 0))
        scratch = [pltpu.VMEM((rows, LINE), jnp.float32)]
    else:
        last = jax.ShapeDtypeStruct((rows, LINE), jnp.float32)
        last_spec = lines
        scratch = []
    return pl.pallas_call(
        functools.partial(head_kernel, pieces, steps, features, resumed, finished),
        grid=(steps,),
        in_specs=in_specs,
        out_specs=[whole, whole, last_spec],
        out_shape=[logits, logits, last],
        scratch_shapes=scratch,
        compiler_params=params(26),
        cost_estimate=pl.CostEstimate(
            flops=4 * rows * blocks * LINE * columns,
            bytes_accessed=4 * blocks * LINE * columns,
            transcendentals=0,
        ),
        name="expert_head",
    )(*gathered, own_weight, other_weight, gain, *(before or ()))


def amateur_kernel(place_ref, hidden_ref, weight_ref, logits_ref, stats_ref):
    logits = jnp.dot(
        hidden_ref[...], weight_ref[...], preferred_element_type=jnp.float32
    ).astype(jnp.bfloat16)
    logits_ref[...] = logits
    wide = logits.astype(jnp.float32)
    largest = jnp.max(wide, axis=1, keepdims=True)
    totals = jnp.sum(jnp.exp(wide - largest), axis=1, keepdims=True)
    for plane in range(2):
        picks = range(plane * 8, wide.shape[0], 16)
        stats_ref[0, plane] = laid_along_lanes(
            jnp.concatenate([largest[at : at + 8] for at in picks], axis=0),
            jnp.concatenate([totals[at : at + 8] for at in picks], axis=0),
        )


def amateur_logits(hidden, weight, place, columns):
    rows, width = hidden.shape
    tall = 2 * LINE
    return pl.pallas_call(
        amateur_kernel,
        grid_spec=pltpu.PrefetchScalarGridSpec(
            num_scalar_prefetch=1,
            grid=(rows // tall,),
            in_specs=[
                pl.BlockSpec((tall, width), lambda i, place: (i, 0)),
                pl.BlockSpec((width, columns), lambda i, place: (0, place[0])),
            ],
            out_specs=[
                pl.BlockSpec((tall, columns), lambda i, place: (i, 0)),
                pl.BlockSpec((1, 2, 2, LINE), lambda i, place: (i, 0, 0, 0)),
            ],
        ),
        out_shape=[
            pltpu.HBM((rows, columns), jnp.bfloat16),
            jax.ShapeDtypeStruct((rows // tall, 2, 2, LINE), jnp.float32),
        ],
        compiler_params=params(16),
        cost_estimate=pl.CostEstimate(
            flops=2 * rows * width * columns,
            bytes_accessed=2 * (rows * width + width * columns + rows * columns),
            transcendentals=rows * columns,
        ),
        name="amateur_head",
    )(place, hidden, weight)


def merged(parts):
    largest = jnp.max(parts[:, :, 0], axis=0)
    totals = jnp.sum(parts[:, :, 1] * jnp.exp(parts[:, :, 0] - largest[None]), axis=0)
    return largest, totals


def spread_kernel(
    place_ref, first_ref, rest_ref, amateur_ref, out_ref, stats_ref, group_ref, sem
):
    quarters = amateur_ref.shape[0] // 2
    for piece in range(quarters):
        at = pl.ds(2 * lax.rem(place_ref[0] + piece, quarters), 2)
        stats_ref[at] = first_ref[...] if piece == 0 else rest_ref[2 * piece - 2 : 2 * piece]
    stats_ref[2 * quarters :] = amateur_ref[...]
    for target in range(group_ref.shape[0]):
        group_ref[target] = stats_ref[...]
    many = group_ref.shape[0]
    copies = [
        pltpu.make_async_copy(group_ref, out_ref.at[pl.ds(at, many)], sem.at[at // many])
        for at in range(0, out_ref.shape[0], many)
    ]
    for copy in copies:
        copy.start()
    for copy in copies:
        copy.wait()


def spread(place, first, rest, amateur, targets):
    rows = 2 * amateur.shape[0]
    vmem = pl.BlockSpec(memory_space=pltpu.VMEM)
    return pl.pallas_call(
        spread_kernel,
        in_specs=[pl.BlockSpec(memory_space=pltpu.SMEM)] + [vmem] * 3,
        out_specs=pl.BlockSpec(memory_space=pltpu.HBM),
        out_shape=pltpu.HBM((targets, rows, LINE), jnp.float32),
        scratch_shapes=[
            pltpu.VMEM((rows, LINE), jnp.float32),
            pltpu.VMEM((8, rows, LINE), jnp.float32),
            pltpu.SemaphoreType.DMA((targets // 8,)),
        ],
        compiler_params=params(4),
        name="spread_stats",
    )(place, first, rest, amateur)


def merge_kernel(parts_ref, out_ref):
    parts = parts_ref[...]
    largest = jnp.max(parts, axis=0)
    quarters = out_ref.shape[0] // 2
    tops, sums = [], []
    for tile in range(2 * quarters):
        top = largest[2 * tile : 2 * tile + 1]
        scales = jnp.exp(parts[:, 2 * tile] - top)
        tops.append(top)
        sums.append(
            top + jnp.log(jnp.sum(parts[:, 2 * tile + 1] * scales, axis=0, keepdims=True))
        )
    shifts = [sums[tile] - sums[quarters + tile] for tile in range(quarters)]
    out_ref[...] = jnp.concatenate(tops[:quarters] + shifts, axis=0)


def merge(parts):
    return pl.pallas_call(
        merge_kernel,
        out_shape=jax.ShapeDtypeStruct((parts.shape[1] // 2, LINE), jnp.float32),
        compiler_params=params(8),
        name="merge_stats",
    )(parts)


def column_of(row):
    return jnp.transpose(jnp.broadcast_to(row, (LINE, LINE)))


def contrast_kernel(
    place_ref,
    mine_ref,
    theirs_ref,
    limit_ref,
    own_first_in,
    own_rest_in,
    other_first_in,
    other_rest_in,
    amateur_in,
    out_ref,
    own_first,
    own_rest,
    other_first,
    other_rest,
    amateur_ref,
    result_ref,
    sem,
    sem_in,
):
    arrivals = [
        pltpu.make_async_copy(source, target, sem_in.at[i])
        for i, (source, target) in enumerate(
            (
                (own_first_in, own_first),
                (other_first_in, other_first),
                (amateur_in, amateur_ref),
                (own_rest_in, own_rest),
                (other_rest_in, other_rest),
            )
        )
    ]
    for copy in arrivals:
        copy.start()
    core = place_ref[1]
    first = core == 0
    quarters = limit_ref.shape[0] // 2
    tall = 2 * LINE
    step_rows = 32
    copies = []
    for piece in range(quarters):
        quarter = lax.rem(place_ref[0] + piece, quarters)
        start = pl.multiple_of(quarter * tall, tall)
        sides = []
        for stats, plane in ((mine_ref, core), (theirs_ref, 1 - core)):
            top = stats[pl.ds(quarter, 1)]
            limit = limit_ref[pl.ds(plane * quarters + quarter, 1)]
            sides.append(
                (column_of(limit - top), column_of(stats[pl.ds(quarters + quarter, 1)]))
            )
        for copy in (arrivals[:3], arrivals[3:], (), ())[piece]:
            copy.wait()
        experts = (own_first, other_first) if piece == 0 else (own_rest, other_rest)
        offset = 0 if piece == 0 else (piece - 1) * LINE
        for at in range(0, LINE, step_rows):
            rows = slice(at, at + step_rows)
            own, other = (
                expert - shift[rows, :1] + jnp.minimum(expert + limit[rows, :1], 0.0)
                for expert, (limit, shift) in zip(
                    (ref[offset + at : offset + at + step_rows] for ref in experts), sides
                )
            )
            planes = (jnp.where(first, own, other), jnp.where(first, other, own))
            mixed = jnp.concatenate(
                [plane[i : i + 8] for i in range(0, step_rows, 8) for plane in planes], axis=0
            )
            amateur = amateur_ref[pl.ds(pl.multiple_of(start + 2 * at, 2 * step_rows), 2 * step_rows)]
            result_ref[piece, 2 * at : 2 * at + 2 * step_rows] = mixed - amateur.astype(jnp.float32)
        copy = pltpu.make_async_copy(
            result_ref.at[piece], out_ref.at[pl.ds(start, tall)], sem.at[piece]
        )
        copy.start()
        copies.append(copy)
    for copy in copies:
        copy.wait()


def contrast(place, mine, theirs, limit, own, other, amateur):
    rows, columns = amateur.shape
    vmem = pl.BlockSpec(memory_space=pltpu.VMEM)
    return pl.pallas_call(
        contrast_kernel,
        in_specs=[pl.BlockSpec(memory_space=pltpu.SMEM)]
        + [vmem] * 3
        + [pl.BlockSpec(memory_space=pl.ANY)] * 5,
        out_specs=pl.BlockSpec(memory_space=pl.ANY),
        out_shape=jax.ShapeDtypeStruct((rows, columns), jnp.float32),
        scratch_shapes=[pltpu.VMEM(a.shape, a.dtype) for a in (*own, *other, amateur)]
        + [
            pltpu.VMEM((rows // (2 * LINE), 2 * LINE, columns), jnp.float32),
            pltpu.SemaphoreType.DMA((rows // (2 * LINE),)),
            pltpu.SemaphoreType.DMA((5,)),
        ],
        compiler_params=params(60),
        cost_estimate=pl.CostEstimate(
            flops=6 * rows * columns, bytes_accessed=10 * rows * columns, transcendentals=0
        ),
        name="contrast",
    )(place, mine, theirs, limit, own[0], own[1], other[0], other[1], amateur)


def body(
    queries,
    cache_keys,
    cache_values,
    new_keys,
    new_values,
    lengths,
    residual,
    gain,
    out_weight,
    head_weight,
    amateur_hidden,
    amateur_head,
    thresholds,
):
    z, y, x = (lax.axis_index(axis) for axis in CHIPS)
    core = lax.axis_index("core")
    first = core == 0
    sizes = tuple(lax.axis_size(axis) for axis in CHIPS)
    depth, chips = sizes[0], int(np.prod(sizes))
    per, width = queries.shape
    rows = residual.shape[0]
    columns = head_weight.shape[1]
    slab = width // depth
    heads = QH // depth
    quarter = quarter_of(z, y, x)

    attention = attend(queries, cache_keys, cache_values, new_keys, new_values, lengths)
    slabs = attention.reshape(per, depth, heads, LINE).transpose(1, 2, 0, 3)
    copies = jnp.broadcast_to(
        slabs.reshape(depth, 1, heads * per, LINE), (depth, chips // depth, heads * per, LINE)
    ).reshape(chips * heads * per, LINE)
    copies, residual, kept_weight = lax.optimization_barrier((copies, residual, out_weight))
    everyone = lax.all_gather(amateur_hidden, "z", axis=0, tiled=True)
    arrived = lax.all_to_all(copies, CHIPS, split_axis=0, concat_axis=0, tiled=True)

    other_weight = shift(head_weight, "core", 1)

    pieces = []
    for step in range(depth):
        turned = (kept_weight if step == 0 else out_weight).T
        part = lax.dynamic_slice_in_dim(turned, lax.rem(z + step, depth) * slab, slab, 1)
        pieces.append(part if step == 0 else shift(part, "z", step))
    mine = jnp.stack(pieces)
    theirs = shift(mine, "core", 1)
    projection = jnp.stack(
        [jnp.where(first, mine, theirs), jnp.where(first, theirs, mine)], axis=1
    ).reshape(depth * 2 * turned.shape[0], slab)

    planes = residual.T.reshape(-1, chips, 2, per)
    kept = lax.dynamic_index_in_dim(planes, core, 2, False)
    given = shift(lax.dynamic_index_in_dim(planes, 1 - core, 2, False), "core", 1)
    base = jnp.concatenate([jnp.where(first, kept, given), jnp.where(first, given, kept)], axis=0)
    base = base.reshape(-1, chips * per).T

    left = arrived.reshape(chips, heads, per, LINE).transpose(0, 2, 1, 3).reshape(chips * per, slab)
    projection = pltpu.with_memory_space_constraint(projection, pltpu.HBM)
    total, *sent = project(left, projection, base)
    parts = [shift(part, "z", -step) for step, part in enumerate(sent, 1)]
    total, everyone = lax.optimization_barrier((total, everyone))

    turns = [quarter_of(*place, 0) for place in np.ndindex(*sizes[:2])]
    copies = hidden_copies(total, parts, turns).reshape(chips, LINE, LINE)
    quarters = lax.all_to_all(copies, CHIPS, split_axis=0, concat_axis=0, tiled=True)
    amateur, amateur_stats = amateur_logits(everyone, amateur_head, z.reshape(1), columns)
    by_plane = amateur_stats.transpose(1, 0, 2, 3)
    kept = lax.dynamic_index_in_dim(by_plane, core, 0, False)
    given = shift(lax.dynamic_index_in_dim(by_plane, 1 - core, 0, False), "core", 1)
    amateur_chip = jnp.stack(merged(jnp.stack([kept, given])), axis=1)

    limit = thresholds.astype(jnp.float32).reshape(chips, 2, per).transpose(1, 0, 2)
    limit = limit.reshape(rows // LINE, LINE) * LOG_TWO
    place = jnp.stack([quarter, core])
    quarters, amateur, amateur_chip, limit, place = lax.optimization_barrier(
        (quarters, amateur, amateur_chip, limit, place)
    )
    moves = (
        ((0, 0, -1), (-1, 0, 0)),
        ((0, -1, 0), (0, 1, 0)),
        ((0, 0, 1), (1, 0, 0)),
    )
    half = chips * 6 // 8

    gain_lines = gain.reshape(-1, LINE)
    halves = [[shift_chips(quarters[:half], move) for move in moves]]
    halves.append([shift_chips(quarters[half:], move) for move in moves[:2]])
    far = [pltpu.with_memory_space_constraint(w, pltpu.HBM) for w in (head_weight, other_weight)]
    own_0, other_0, stats_0 = head([quarters], *far, gain_lines)
    later, own_0 = lax.optimization_barrier((quarters[half:], own_0))
    halves[1].append(shift_chips(later, moves[2]))
    begun = head(halves[0], head_weight, other_weight, gain_lines, finished=False)
    own_1, other_1, stats_1 = head(
        halves[1], head_weight, other_weight, gain_lines, start=half, before=begun
    )
    crossed = [shift(logits, "core", 1) for logits in (other_0, other_1)]

    copies = spread(place, stats_0, stats_1, amateur_chip.reshape(-1, LINE), chips)
    mine = merge(lax.all_to_all(copies, CHIPS, split_axis=0, concat_axis=0, tiled=True))
    theirs = shift(mine, "core", 1)
    return contrast(place, mine, theirs, limit, (own_0, own_1), crossed, amateur)


def solution(mesh):
    fine = Mesh(mesh.devices.reshape(4, 4, 4, 2), ALL)
    every = ALL
    by_vocab = ("y", "x", "core")
    in_specs = (
        P(every, None),
        P(every, None, None),
        P(every, None, None),
        P(every, None),
        P(every, None),
        P(every),
        P(None, every),
        P(),
        P(None, every),
        P(None, by_vocab + ("z",)),
        P("z", None),
        P(None, by_vocab),
        P(),
    )
    out_specs = P(None, by_vocab + ("z",))
    return jax.shard_map(body, mesh=fine, in_specs=in_specs, out_specs=out_specs, check_vma=False)
```

```python
import functools
import math

import jax
import jax.numpy as jnp
import numpy as np
from jax import lax
from jax.experimental import pallas as pl
from jax.experimental.pallas import tpu as pltpu
from jax.sharding import Mesh
from jax.sharding import PartitionSpec as P

QH = 64
KVH = 8

EPSILON = 1e-06
LOG_TWO = math.log(2.0)
MASK_FILL = -1e30

CHIPS = ("z", "y", "x")
ALL = ("z", "y", "x", "core")
LINE = 128


def attend(queries, cache_keys, cache_values, new_keys, new_values, lengths):
    row_count = queries.shape[0]
    positions = cache_keys.shape[1]
    head_size = queries.shape[1] // QH
    groups = QH // KVH
    scaling = head_size ** (-0.5)
    query_block = queries.reshape(row_count, KVH, groups, head_size)
    key_block = cache_keys.reshape(row_count, positions, KVH, head_size)
    value_block = cache_values.reshape(row_count, positions, KVH, head_size)
    scores = (
        jnp.einsum("rkgd,rlkd->rkgl", query_block, key_block, preferred_element_type=jnp.float32)
        * scaling
    )
    own_score = (
        jnp.einsum(
            "rkgd,rkd->rkg",
            query_block,
            new_keys.reshape(row_count, KVH, head_size),
            preferred_element_type=jnp.float32,
        )
        * scaling
    )
    live_mask = (jnp.arange(positions, dtype=jnp.int32)[None, :] < lengths[:, None])[
        :, None, None, :
    ]
    scores = jnp.where(live_mask, scores, MASK_FILL)
    largest = jnp.maximum(jnp.max(scores, axis=-1), own_score)
    weights = jnp.where(live_mask, jnp.exp(scores - largest[..., None]), 0.0)
    own_weight = jnp.exp(own_score - largest)
    totals = jnp.sum(weights, axis=-1) + own_weight
    probabilities = (weights / totals[..., None]).astype(jnp.bfloat16)
    own_probability = (own_weight / totals).astype(jnp.bfloat16)
    mixture = jnp.einsum(
        "rkgl,rlkd->rkgd", probabilities, value_block, preferred_element_type=jnp.float32
    )
    mixture = mixture + own_probability.astype(jnp.float32)[..., None] * new_values.reshape(
        row_count, KVH, 1, head_size
    ).astype(jnp.float32)
    return mixture.reshape(row_count, QH, head_size).astype(jnp.bfloat16)


def shift(x, axis, step):
    size = lax.axis_size(axis)
    return lax.ppermute(x, axis, [(i, (i + step) % size) for i in range(size)])


def shift_chips(x, offsets):
    sizes = tuple(lax.axis_size(axis) for axis in ALL)
    pairs = []
    for place in np.ndindex(*sizes):
        offset = offsets[place[3]] + (0,)
        target = tuple((a + o) % s for a, o, s in zip(place, offset, sizes))
        pairs.append(
            (int(np.ravel_multi_index(place, sizes)), int(np.ravel_multi_index(target, sizes)))
        )
    return lax.ppermute(x, ALL, pairs)


def quarter_of(z, y, x):
    return (x + 2 * y + z) % 4


def params(mebibytes):
    return pltpu.CompilerParams(vmem_limit_bytes=mebibytes * 1024 * 1024)


def laid_along_lanes(largest, totals):
    lane = lax.broadcasted_iota(jnp.int32, (LINE, LINE), 1)
    return jnp.transpose(jnp.where(lane == 0, largest, totals))[:2]


def projection_kernel(left_ref, weight_ref, base_ref, total_ref, *sent):
    product = lax.dot_general(
        left_ref[...],
        weight_ref[...],
        (((1,), (1,)), ((), ())),
        preferred_element_type=jnp.float32,
    )
    total_ref[...] = base_ref[...].astype(jnp.float32) + product[:, :LINE]
    for step, sent_ref in enumerate(sent, 1):
        sent_ref[...] = product[:, step * LINE : (step + 1) * LINE].astype(jnp.bfloat16)


def project(left, weight, base):
    rows, depth = left.shape
    columns = weight.shape[0]
    return pl.pallas_call(
        projection_kernel,
        out_shape=[jax.ShapeDtypeStruct((rows, LINE), jnp.float32)]
        + [jax.ShapeDtypeStruct((rows, LINE), jnp.bfloat16)] * (columns // LINE - 1),
        compiler_params=params(16),
        cost_estimate=pl.CostEstimate(
            flops=2 * rows * depth * columns,
            bytes_accessed=2 * (rows + columns) * depth,
            transcendentals=0,
        ),
        name="projection",
    )(left, weight, base)


def hidden_kernel(turns, total_ref, *refs):
    parts, out_ref, hidden_ref, sem = refs[:-3], refs[-3], refs[-2], refs[-1]
    total = total_ref[...]
    for part in parts:
        total = total + part[...].astype(jnp.float32)
    hidden = total.astype(jnp.bfloat16)
    rows = hidden.shape[0]
    hidden_ref[:rows] = hidden
    hidden_ref[rows:] = hidden
    copies = [
        pltpu.make_async_copy(
            hidden_ref.at[pl.ds(turn * LINE, rows)], out_ref.at[line], sem.at[line]
        )
        for line, turn in enumerate(turns)
    ]
    for copy in copies:
        copy.start()
    for copy in copies:
        copy.wait()


def hidden_copies(total, parts, turns):
    rows = total.shape[0]
    return pl.pallas_call(
        functools.partial(hidden_kernel, turns),
        out_specs=pl.BlockSpec(memory_space=pltpu.HBM),
        out_shape=pltpu.HBM((len(turns), rows, LINE), jnp.bfloat16),
        scratch_shapes=[
            pltpu.VMEM((2 * rows, LINE), jnp.bfloat16),
            pltpu.SemaphoreType.DMA((len(turns),)),
        ],
        compiler_params=params(8),
        name="hidden",
    )(total, *parts)


def head_kernel(pieces, steps, features, resumed, finished, *refs):
    refs = list(refs)
    gathered = [refs.pop(0) for _ in range(pieces)]
    own_weight, other_weight, gain_ref = [refs.pop(0) for _ in range(3)]
    if resumed:
        own_before, other_before, squares_before = [refs.pop(0) for _ in range(3)]
    own_ref, other_ref, last_ref = [refs.pop(0) for _ in range(3)]
    squares_ref = refs.pop(0) if finished else last_ref
    step = pl.program_id(0)

    @pl.when(step == 0)
    def _():
        own_ref[...] = own_before[...] if resumed else jnp.zeros_like(own_ref)
        other_ref[...] = other_before[...] if resumed else jnp.zeros_like(other_ref)
        squares_ref[...] = squares_before[...] if resumed else jnp.zeros_like(squares_ref)

    rows = []
    for piece in range(pieces):
        blocks = []
        squares = None
        for block in range(gathered[piece].shape[0]):
            wide = gathered[piece][block].astype(jnp.float32)
            squares = wide * wide if squares is None else squares + wide * wide
            blocks.append((wide * gain_ref[block : block + 1]).astype(jnp.bfloat16))
        rows.append(jnp.concatenate(blocks, axis=1))
        squares_ref[piece * LINE : piece * LINE + LINE] += squares
    left = jnp.concatenate(rows, axis=0)
    own_ref[...] += jnp.dot(left, own_weight[...], preferred_element_type=jnp.float32)
    other_ref[...] += jnp.dot(left, other_weight[...], preferred_element_type=jnp.float32)

    if finished:

        @pl.when(step == steps - 1)
        def _():
            for piece in range(pieces):
                tile = slice(piece * LINE, piece * LINE + LINE)
                mean = jnp.sum(squares_ref[tile], axis=1, keepdims=True) / features
                scale = lax.rsqrt(mean + EPSILON)
                own = own_ref[tile] * scale
                other = other_ref[tile] * scale
                own_ref[tile] = own
                other_ref[tile] = other
                largest = jnp.maximum(
                    jnp.max(own, axis=1, keepdims=True), jnp.max(other, axis=1, keepdims=True)
                )
                totals = jnp.sum(jnp.exp(own - largest), axis=1, keepdims=True) + jnp.sum(
                    jnp.exp(other - largest), axis=1, keepdims=True
                )
                last_ref[2 * piece : 2 * piece + 2] = laid_along_lanes(largest, totals)


def head(gathered, own_weight, other_weight, gain, start=0, before=None, finished=True):
    pieces = len(gathered)
    blocks = gathered[0].shape[0]
    features, columns = own_weight.shape
    per = 8
    steps = blocks // per
    first = start // per
    rows = pieces * LINE
    resumed = before is not None
    whole = pl.BlockSpec((rows, columns), lambda i: (0, 0))
    lines = pl.BlockSpec((rows, LINE), lambda i: (0, 0))
    weight = pl.BlockSpec((per * LINE, columns), lambda i: (i + first, 0))
    in_specs = [pl.BlockSpec((per, LINE, LINE), lambda i: (i, 0, 0))] * pieces + [
        weight,
        weight,
        pl.BlockSpec((per, LINE), lambda i: (i + first, 0)),
    ]
    if resumed:
        in_specs += [whole, whole, lines]
    logits = jax.ShapeDtypeStruct((rows, columns), jnp.float32)
    if finished:
        logits = pltpu.HBM(logits.shape, logits.dtype)
        last = jax.ShapeDtypeStruct((2 * pieces, LINE), jnp.float32)
        last_spec = pl.BlockSpec((2 * pieces, LINE), lambda i: (0, 0))
        scratch = [pltpu.VMEM((rows, LINE), jnp.float32)]
    else:
        last = jax.ShapeDtypeStruct((rows, LINE), jnp.float32)
        last_spec = lines
        scratch = []
    return pl.pallas_call(
        functools.partial(head_kernel, pieces, steps, features, resumed, finished),
        grid=(steps,),
        in_specs=in_specs,
        out_specs=[whole, whole, last_spec],
        out_shape=[logits, logits, last],
        scratch_shapes=scratch,
        compiler_params=params(26),
        cost_estimate=pl.CostEstimate(
            flops=4 * rows * blocks * LINE * columns,
            bytes_accessed=4 * blocks * LINE * columns,
            transcendentals=0,
        ),
        name="expert_head",
    )(*gathered, own_weight, other_weight, gain, *(before or ()))


def amateur_kernel(place_ref, hidden_ref, weight_ref, logits_ref, stats_ref):
    logits = jnp.dot(
        hidden_ref[...], weight_ref[...], preferred_element_type=jnp.float32
    ).astype(jnp.bfloat16)
    logits_ref[...] = logits
    wide = logits.astype(jnp.float32)
    largest = jnp.max(wide, axis=1, keepdims=True)
    totals = jnp.sum(jnp.exp(wide - largest), axis=1, keepdims=True)
    for plane in range(2):
        picks = range(plane * 8, wide.shape[0], 16)
        stats_ref[0, plane] = laid_along_lanes(
            jnp.concatenate([largest[at : at + 8] for at in picks], axis=0),
            jnp.concatenate([totals[at : at + 8] for at in picks], axis=0),
        )


def amateur_logits(hidden, weight, place, columns):
    rows, width = hidden.shape
    tall = 2 * LINE
    return pl.pallas_call(
        amateur_kernel,
        grid_spec=pltpu.PrefetchScalarGridSpec(
            num_scalar_prefetch=1,
            grid=(rows // tall,),
            in_specs=[
                pl.BlockSpec((tall, width), lambda i, place: (i, 0)),
                pl.BlockSpec((width, columns), lambda i, place: (0, place[0])),
            ],
            out_specs=[
                pl.BlockSpec((tall, columns), lambda i, place: (i, 0)),
                pl.BlockSpec((1, 2, 2, LINE), lambda i, place: (i, 0, 0, 0)),
            ],
        ),
        out_shape=[
            pltpu.HBM((rows, columns), jnp.bfloat16),
            jax.ShapeDtypeStruct((rows // tall, 2, 2, LINE), jnp.float32),
        ],
        compiler_params=params(16),
        cost_estimate=pl.CostEstimate(
            flops=2 * rows * width * columns,
            bytes_accessed=2 * (rows * width + width * columns + rows * columns),
            transcendentals=rows * columns,
        ),
        name="amateur_head",
    )(place, hidden, weight)


def merged(parts):
    largest = jnp.max(parts[:, :, 0], axis=0)
    totals = jnp.sum(parts[:, :, 1] * jnp.exp(parts[:, :, 0] - largest[None]), axis=0)
    return largest, totals


def spread_kernel(
    place_ref, first_ref, rest_ref, amateur_ref, out_ref, stats_ref, group_ref, sem
):
    quarters = amateur_ref.shape[0] // 2
    for piece in range(quarters):
        at = pl.ds(2 * lax.rem(place_ref[0] + piece, quarters), 2)
        stats_ref[at] = first_ref[...] if piece == 0 else rest_ref[2 * piece - 2 : 2 * piece]
    amateur = amateur_ref[...]
    rows = []
    for quarter in range(quarters):
        at = 2 * quarter
        largest = stats_ref[at : at + 1]
        coarse = largest.astype(jnp.bfloat16).astype(jnp.float32)
        amateur_lse = amateur[at : at + 1] + jnp.log(amateur[at + 1 : at + 2])
        rows += [
            coarse,
            largest - coarse,
            stats_ref[at + 1 : at + 2],
            amateur_lse - largest,
        ]
    packed = jnp.concatenate(rows, axis=0).astype(jnp.bfloat16)
    many = group_ref.shape[0]
    for target in range(many):
        group_ref[target] = packed
    copies = [
        pltpu.make_async_copy(group_ref, out_ref.at[pl.ds(at, many)], sem.at[at // many])
        for at in range(0, out_ref.shape[0], many)
    ]
    for copy in copies:
        copy.start()
    for copy in copies:
        copy.wait()


def spread(place, first, rest, amateur, targets):
    rows = 2 * amateur.shape[0]
    many = 16
    vmem = pl.BlockSpec(memory_space=pltpu.VMEM)
    return pl.pallas_call(
        spread_kernel,
        in_specs=[pl.BlockSpec(memory_space=pltpu.SMEM)] + [vmem] * 3,
        out_specs=pl.BlockSpec(memory_space=pltpu.HBM),
        out_shape=pltpu.HBM((targets, rows, LINE), jnp.bfloat16),
        scratch_shapes=[
            pltpu.VMEM(amateur.shape, jnp.float32),
            pltpu.VMEM((many, rows, LINE), jnp.bfloat16),
            pltpu.SemaphoreType.DMA((targets // many,)),
        ],
        compiler_params=params(4),
        name="spread_stats",
    )(place, first, rest, amateur)


def merge_kernel(parts_ref, out_ref):
    parts = parts_ref[...].astype(jnp.float32)
    tops, shifts = [], []
    for quarter in range(out_ref.shape[0] // 2):
        coarse, fine, sums, apart = (parts[:, 4 * quarter + i] for i in range(4))
        largest = coarse + fine
        amateur = largest + apart
        top = jnp.max(largest, axis=0, keepdims=True)
        amateur_top = jnp.max(amateur, axis=0, keepdims=True)
        total = jnp.sum(sums * jnp.exp(largest - top), axis=0, keepdims=True)
        amateur_total = jnp.sum(jnp.exp(amateur - amateur_top), axis=0, keepdims=True)
        tops.append(top)
        shifts.append((top + jnp.log(total)) - (amateur_top + jnp.log(amateur_total)))
    out_ref[...] = jnp.concatenate(tops + shifts, axis=0)


def merge(parts):
    return pl.pallas_call(
        merge_kernel,
        out_shape=jax.ShapeDtypeStruct((parts.shape[1] // 2, LINE), jnp.float32),
        compiler_params=params(8),
        name="merge_stats",
    )(parts)


def column_of(row):
    return jnp.transpose(jnp.broadcast_to(row, (LINE, LINE)))


def contrast_kernel(
    place_ref,
    mine_ref,
    theirs_ref,
    limit_ref,
    own_first_in,
    own_rest_in,
    other_first_in,
    other_rest_in,
    amateur_in,
    out_ref,
    own_first,
    own_rest,
    other_first,
    other_rest,
    amateur_ref,
    result_ref,
    sem,
    sem_in,
):
    arrivals = [
        pltpu.make_async_copy(source, target, sem_in.at[i])
        for i, (source, target) in enumerate(
            (
                (own_first_in, own_first),
                (other_first_in, other_first),
                (amateur_in, amateur_ref),
                (own_rest_in, own_rest),
                (other_rest_in, other_rest),
            )
        )
    ]
    for copy in arrivals:
        copy.start()
    core = place_ref[1]
    first = core == 0
    quarters = limit_ref.shape[0] // 2
    tall = 2 * LINE
    step_rows = 32
    copies = []
    for piece in range(quarters):
        quarter = lax.rem(place_ref[0] + piece, quarters)
        start = pl.multiple_of(quarter * tall, tall)
        sides = []
        for stats, plane in ((mine_ref, core), (theirs_ref, 1 - core)):
            top = stats[pl.ds(quarter, 1)]
            limit = limit_ref[pl.ds(plane * quarters + quarter, 1)]
            sides.append(
                (column_of(limit - top), column_of(stats[pl.ds(quarters + quarter, 1)]))
            )
        for copy in (arrivals[:3], arrivals[3:], (), ())[piece]:
            copy.wait()
        experts = (own_first, other_first) if piece == 0 else (own_rest, other_rest)
        offset = 0 if piece == 0 else (piece - 1) * LINE
        for at in range(0, LINE, step_rows):
            rows = slice(at, at + step_rows)
            own, other = (
                expert - shift[rows, :1] + jnp.minimum(expert + limit[rows, :1], 0.0)
                for expert, (limit, shift) in zip(
                    (ref[offset + at : offset + at + step_rows] for ref in experts), sides
                )
            )
            planes = (jnp.where(first, own, other), jnp.where(first, other, own))
            mixed = jnp.concatenate(
                [plane[i : i + 8] for i in range(0, step_rows, 8) for plane in planes], axis=0
            )
            amateur = amateur_ref[pl.ds(pl.multiple_of(start + 2 * at, 2 * step_rows), 2 * step_rows)]
            result_ref[piece, 2 * at : 2 * at + 2 * step_rows] = mixed - amateur.astype(jnp.float32)
        copy = pltpu.make_async_copy(
            result_ref.at[piece], out_ref.at[pl.ds(start, tall)], sem.at[piece]
        )
        copy.start()
        copies.append(copy)
    for copy in copies:
        copy.wait()


def contrast(place, mine, theirs, limit, own, other, amateur):
    rows, columns = amateur.shape
    vmem = pl.BlockSpec(memory_space=pltpu.VMEM)
    return pl.pallas_call(
        contrast_kernel,
        in_specs=[pl.BlockSpec(memory_space=pltpu.SMEM)]
        + [vmem] * 3
        + [pl.BlockSpec(memory_space=pl.ANY)] * 5,
        out_specs=pl.BlockSpec(memory_space=pl.ANY),
        out_shape=jax.ShapeDtypeStruct((rows, columns), jnp.float32),
        scratch_shapes=[pltpu.VMEM(a.shape, a.dtype) for a in (*own, *other, amateur)]
        + [
            pltpu.VMEM((rows // (2 * LINE), 2 * LINE, columns), jnp.float32),
            pltpu.SemaphoreType.DMA((rows // (2 * LINE),)),
            pltpu.SemaphoreType.DMA((5,)),
        ],
        compiler_params=params(60),
        cost_estimate=pl.CostEstimate(
            flops=6 * rows * columns, bytes_accessed=10 * rows * columns, transcendentals=0
        ),
        name="contrast",
    )(place, mine, theirs, limit, own[0], own[1], other[0], other[1], amateur)


def body(
    queries,
    cache_keys,
    cache_values,
    new_keys,
    new_values,
    lengths,
    residual,
    gain,
    out_weight,
    head_weight,
    amateur_hidden,
    amateur_head,
    thresholds,
):
    z, y, x = (lax.axis_index(axis) for axis in CHIPS)
    core = lax.axis_index("core")
    first = core == 0
    sizes = tuple(lax.axis_size(axis) for axis in CHIPS)
    depth, chips = sizes[0], int(np.prod(sizes))
    per, width = queries.shape
    rows = residual.shape[0]
    columns = head_weight.shape[1]
    slab = width // depth
    heads = QH // depth
    quarter = quarter_of(z, y, x)

    attention = attend(queries, cache_keys, cache_values, new_keys, new_values, lengths)
    slabs = attention.reshape(per, depth, heads, LINE).transpose(1, 2, 0, 3)
    copies = jnp.broadcast_to(
        slabs.reshape(depth, 1, heads * per, LINE), (depth, chips // depth, heads * per, LINE)
    ).reshape(chips * heads * per, LINE)
    copies, residual, kept_weight = lax.optimization_barrier((copies, residual, out_weight))
    everyone = lax.all_gather(amateur_hidden, "z", axis=0, tiled=True)
    arrived = lax.all_to_all(copies, CHIPS, split_axis=0, concat_axis=0, tiled=True)

    other_weight = shift(head_weight, "core", 1)

    pieces = []
    for step in range(depth):
        turned = (kept_weight if step == 0 else out_weight).T
        part = lax.dynamic_slice_in_dim(turned, lax.rem(z + step, depth) * slab, slab, 1)
        pieces.append(part if step == 0 else shift(part, "z", step))
    mine = jnp.stack(pieces)
    theirs = shift(mine, "core", 1)
    projection = jnp.stack(
        [jnp.where(first, mine, theirs), jnp.where(first, theirs, mine)], axis=1
    ).reshape(depth * 2 * turned.shape[0], slab)

    planes = residual.T.reshape(-1, chips, 2, per)
    kept = lax.dynamic_index_in_dim(planes, core, 2, False)
    given = shift(lax.dynamic_index_in_dim(planes, 1 - core, 2, False), "core", 1)
    base = jnp.concatenate([jnp.where(first, kept, given), jnp.where(first, given, kept)], axis=0)
    base = base.reshape(-1, chips * per).T

    left = arrived.reshape(chips, heads, per, LINE).transpose(0, 2, 1, 3).reshape(chips * per, slab)
    projection = pltpu.with_memory_space_constraint(projection, pltpu.HBM)
    total, *sent = project(left, projection, base)
    parts = [shift(part, "z", -step) for step, part in enumerate(sent, 1)]
    total, everyone = lax.optimization_barrier((total, everyone))

    turns = [quarter_of(*place, 0) for place in np.ndindex(*sizes[:2])]
    copies = hidden_copies(total, parts, turns).reshape(chips, LINE, LINE)
    quarters = lax.all_to_all(copies, CHIPS, split_axis=0, concat_axis=0, tiled=True)
    amateur, amateur_stats = amateur_logits(everyone, amateur_head, z.reshape(1), columns)
    by_plane = amateur_stats.transpose(1, 0, 2, 3)
    kept = lax.dynamic_index_in_dim(by_plane, core, 0, False)
    given = shift(lax.dynamic_index_in_dim(by_plane, 1 - core, 0, False), "core", 1)
    amateur_chip = jnp.stack(merged(jnp.stack([kept, given])), axis=1)

    limit = thresholds.astype(jnp.float32).reshape(chips, 2, per).transpose(1, 0, 2)
    limit = limit.reshape(rows // LINE, LINE) * LOG_TWO
    place = jnp.stack([quarter, core])
    quarters, amateur, amateur_chip, limit, place = lax.optimization_barrier(
        (quarters, amateur, amateur_chip, limit, place)
    )
    moves = (
        ((0, 0, -1), (-1, 0, 0)),
        ((0, -1, 0), (0, 1, 0)),
        ((0, 0, 1), (1, 0, 0)),
    )
    half = chips * 6 // 8

    gain_lines = gain.reshape(-1, LINE)
    halves = [[shift_chips(quarters[:half], move) for move in moves]]
    halves.append([shift_chips(quarters[half:], move) for move in moves[:2]])
    far = [pltpu.with_memory_space_constraint(w, pltpu.HBM) for w in (head_weight, other_weight)]
    own_0, other_0, stats_0 = head([quarters], *far, gain_lines)
    later, own_0 = lax.optimization_barrier((quarters[half:], own_0))
    halves[1].append(shift_chips(later, moves[2]))
    begun = head(halves[0], head_weight, other_weight, gain_lines, finished=False)
    own_1, other_1, stats_1 = head(
        halves[1], head_weight, other_weight, gain_lines, start=half, before=begun
    )
    crossed = [shift(logits, "core", 1) for logits in (other_0, other_1)]

    copies = spread(place, stats_0, stats_1, amateur_chip.reshape(-1, LINE), chips)
    mine = merge(lax.all_to_all(copies, CHIPS, split_axis=0, concat_axis=0, tiled=True))
    theirs = shift(mine, "core", 1)
    return contrast(place, mine, theirs, limit, (own_0, own_1), crossed, amateur)


def solution(mesh):
    fine = Mesh(mesh.devices.reshape(4, 4, 4, 2), ALL)
    every = ALL
    by_vocab = ("y", "x", "core")
    in_specs = (
        P(every, None),
        P(every, None, None),
        P(every, None, None),
        P(every, None),
        P(every, None),
        P(every),
        P(None, every),
        P(),
        P(None, every),
        P(None, by_vocab + ("z",)),
        P("z", None),
        P(None, by_vocab),
        P(),
    )
    out_specs = P(None, by_vocab + ("z",))
    return jax.shard_map(body, mesh=fine, in_specs=in_specs, out_specs=out_specs, check_vma=False)
```

```python
import functools
import math

import jax
import jax.numpy as jnp
import numpy as np
from jax import lax
from jax.experimental import pallas as pl
from jax.experimental.pallas import tpu as pltpu
from jax.sharding import Mesh
from jax.sharding import PartitionSpec as P

QH = 64
KVH = 8

EPSILON = 1e-06
LOG_TWO = math.log(2.0)
MASK_FILL = -1e30

CHIPS = ("z", "y", "x")
ALL = ("z", "y", "x", "core")
LINE = 128


def attend(queries, cache_keys, cache_values, new_keys, new_values, lengths):
    row_count = queries.shape[0]
    positions = cache_keys.shape[1]
    head_size = queries.shape[1] // QH
    groups = QH // KVH
    scaling = head_size ** (-0.5)
    query_block = queries.reshape(row_count, KVH, groups, head_size)
    key_block = cache_keys.reshape(row_count, positions, KVH, head_size)
    value_block = cache_values.reshape(row_count, positions, KVH, head_size)
    scores = (
        jnp.einsum("rkgd,rlkd->rkgl", query_block, key_block, preferred_element_type=jnp.float32)
        * scaling
    )
    own_score = (
        jnp.einsum(
            "rkgd,rkd->rkg",
            query_block,
            new_keys.reshape(row_count, KVH, head_size),
            preferred_element_type=jnp.float32,
        )
        * scaling
    )
    live_mask = (jnp.arange(positions, dtype=jnp.int32)[None, :] < lengths[:, None])[
        :, None, None, :
    ]
    scores = jnp.where(live_mask, scores, MASK_FILL)
    largest = jnp.maximum(jnp.max(scores, axis=-1), own_score)
    weights = jnp.where(live_mask, jnp.exp(scores - largest[..., None]), 0.0)
    own_weight = jnp.exp(own_score - largest)
    totals = jnp.sum(weights, axis=-1) + own_weight
    probabilities = (weights / totals[..., None]).astype(jnp.bfloat16)
    own_probability = (own_weight / totals).astype(jnp.bfloat16)
    mixture = jnp.einsum(
        "rkgl,rlkd->rkgd", probabilities, value_block, preferred_element_type=jnp.float32
    )
    mixture = mixture + own_probability.astype(jnp.float32)[..., None] * new_values.reshape(
        row_count, KVH, 1, head_size
    ).astype(jnp.float32)
    return mixture.reshape(row_count, QH, head_size).astype(jnp.bfloat16)


def shift(x, axis, step):
    size = lax.axis_size(axis)
    return lax.ppermute(x, axis, [(i, (i + step) % size) for i in range(size)])


def shift_chips(x, offsets):
    sizes = tuple(lax.axis_size(axis) for axis in ALL)
    pairs = []
    for place in np.ndindex(*sizes):
        offset = offsets[place[3]] + (0,)
        target = tuple((a + o) % s for a, o, s in zip(place, offset, sizes))
        pairs.append(
            (int(np.ravel_multi_index(place, sizes)), int(np.ravel_multi_index(target, sizes)))
        )
    return lax.ppermute(x, ALL, pairs)


def quarter_of(z, y, x):
    return (x + 2 * y + z) % 4


def params(mebibytes):
    return pltpu.CompilerParams(vmem_limit_bytes=mebibytes * 1024 * 1024)


def laid_along_lanes(largest, totals):
    lane = lax.broadcasted_iota(jnp.int32, (LINE, LINE), 1)
    return jnp.transpose(jnp.where(lane == 0, largest, totals))[:2]


def copies_kernel(slabs_ref, out_ref, many_ref, sem):
    slabs, many = many_ref.shape[:2]
    copies = []
    for slab in range(slabs):
        for i in range(many):
            many_ref[slab, i] = slabs_ref[slab]
        for at in range(0, out_ref.shape[1], many):
            copy = pltpu.make_async_copy(
                many_ref.at[slab], out_ref.at[slab, pl.ds(at, many)], sem.at[slab, at // many]
            )
            copy.start()
            copies.append(copy)
    for copy in copies:
        copy.wait()


def copied(slabs, targets):
    count, rows, lanes = slabs.shape
    many = 4
    return pl.pallas_call(
        copies_kernel,
        out_specs=pl.BlockSpec(memory_space=pltpu.HBM),
        out_shape=pltpu.HBM((count, targets, rows, lanes), slabs.dtype),
        scratch_shapes=[
            pltpu.VMEM((count, many, rows, lanes), slabs.dtype),
            pltpu.SemaphoreType.DMA((count, targets // many)),
        ],
        compiler_params=params(8),
        name="attention_copies",
    )(slabs)


def projection_kernel(left_ref, weight_ref, base_ref, total_ref, *sent):
    product = lax.dot_general(
        left_ref[...],
        weight_ref[...],
        (((1,), (1,)), ((), ())),
        preferred_element_type=jnp.float32,
    )
    total_ref[...] = base_ref[...].astype(jnp.float32) + product[:, :LINE]
    for step, sent_ref in enumerate(sent, 1):
        sent_ref[...] = product[:, step * LINE : (step + 1) * LINE].astype(jnp.bfloat16)


def project(left, weight, base):
    rows, depth = left.shape
    columns = weight.shape[0]
    return pl.pallas_call(
        projection_kernel,
        out_shape=[jax.ShapeDtypeStruct((rows, LINE), jnp.float32)]
        + [jax.ShapeDtypeStruct((rows, LINE), jnp.bfloat16)] * (columns // LINE - 1),
        compiler_params=params(16),
        cost_estimate=pl.CostEstimate(
            flops=2 * rows * depth * columns,
            bytes_accessed=2 * (rows + columns) * depth,
            transcendentals=0,
        ),
        name="projection",
    )(left, weight, base)


def hidden_kernel(turns, total_ref, *refs):
    parts, out_ref, hidden_ref, sem = refs[:-3], refs[-3], refs[-2], refs[-1]
    total = total_ref[...]
    for part in parts:
        total = total + part[...].astype(jnp.float32)
    hidden = total.astype(jnp.bfloat16)
    rows = hidden.shape[0]
    hidden_ref[:rows] = hidden
    hidden_ref[rows:] = hidden
    copies = [
        pltpu.make_async_copy(
            hidden_ref.at[pl.ds(turn * LINE, rows)], out_ref.at[line], sem.at[line]
        )
        for line, turn in enumerate(turns)
    ]
    for copy in copies:
        copy.start()
    for copy in copies:
        copy.wait()


def hidden_copies(total, parts, turns):
    rows = total.shape[0]
    return pl.pallas_call(
        functools.partial(hidden_kernel, turns),
        out_specs=pl.BlockSpec(memory_space=pltpu.HBM),
        out_shape=pltpu.HBM((len(turns), rows, LINE), jnp.bfloat16),
        scratch_shapes=[
            pltpu.VMEM((2 * rows, LINE), jnp.bfloat16),
            pltpu.SemaphoreType.DMA((len(turns),)),
        ],
        compiler_params=params(8),
        name="hidden",
    )(total, *parts)


def head_kernel(pieces, steps, features, resumed, finished, *refs):
    refs = list(refs)
    gathered = [refs.pop(0) for _ in range(pieces)]
    own_weight, other_weight, gain_ref = [refs.pop(0) for _ in range(3)]
    if resumed:
        own_before, other_before, squares_before = [refs.pop(0) for _ in range(3)]
    own_ref, other_ref, last_ref = [refs.pop(0) for _ in range(3)]
    squares_ref = refs.pop(0) if finished else last_ref
    step = pl.program_id(0)

    @pl.when(step == 0)
    def _():
        own_ref[...] = own_before[...] if resumed else jnp.zeros_like(own_ref)
        other_ref[...] = other_before[...] if resumed else jnp.zeros_like(other_ref)
        squares_ref[...] = squares_before[...] if resumed else jnp.zeros_like(squares_ref)

    rows = []
    for piece in range(pieces):
        blocks = []
        squares = None
        for block in range(gathered[piece].shape[0]):
            wide = gathered[piece][block].astype(jnp.float32)
            squares = wide * wide if squares is None else squares + wide * wide
            blocks.append((wide * gain_ref[block : block + 1]).astype(jnp.bfloat16))
        rows.append(jnp.concatenate(blocks, axis=1))
        squares_ref[piece * LINE : piece * LINE + LINE] += squares
    left = jnp.concatenate(rows, axis=0)
    own_ref[...] += jnp.dot(left, own_weight[...], preferred_element_type=jnp.float32)
    other_ref[...] += jnp.dot(left, other_weight[...], preferred_element_type=jnp.float32)

    if finished:

        @pl.when(step == steps - 1)
        def _():
            for piece in range(pieces):
                tile = slice(piece * LINE, piece * LINE + LINE)
                mean = jnp.sum(squares_ref[tile], axis=1, keepdims=True) / features
                scale = lax.rsqrt(mean + EPSILON)
                own = own_ref[tile] * scale
                other = other_ref[tile] * scale
                own_ref[tile] = own
                other_ref[tile] = other
                largest = jnp.maximum(
                    jnp.max(own, axis=1, keepdims=True), jnp.max(other, axis=1, keepdims=True)
                )
                totals = jnp.sum(jnp.exp(own - largest), axis=1, keepdims=True) + jnp.sum(
                    jnp.exp(other - largest), axis=1, keepdims=True
                )
                last_ref[2 * piece : 2 * piece + 2] = laid_along_lanes(largest, totals)


def head(gathered, own_weight, other_weight, gain, start=0, before=None, finished=True):
    pieces = len(gathered)
    blocks = gathered[0].shape[0]
    features, columns = own_weight.shape
    per = 8
    steps = blocks // per
    first = start // per
    rows = pieces * LINE
    resumed = before is not None
    whole = pl.BlockSpec((rows, columns), lambda i: (0, 0))
    lines = pl.BlockSpec((rows, LINE), lambda i: (0, 0))
    weight = pl.BlockSpec((per * LINE, columns), lambda i: (i + first, 0))
    in_specs = [pl.BlockSpec((per, LINE, LINE), lambda i: (i, 0, 0))] * pieces + [
        weight,
        weight,
        pl.BlockSpec((per, LINE), lambda i: (i + first, 0)),
    ]
    if resumed:
        in_specs += [whole, whole, lines]
    logits = jax.ShapeDtypeStruct((rows, columns), jnp.float32)
    if finished:
        logits = pltpu.HBM(logits.shape, logits.dtype)
        last = jax.ShapeDtypeStruct((2 * pieces, LINE), jnp.float32)
        last_spec = pl.BlockSpec((2 * pieces, LINE), lambda i: (0, 0))
        scratch = [pltpu.VMEM((rows, LINE), jnp.float32)]
    else:
        last = jax.ShapeDtypeStruct((rows, LINE), jnp.float32)
        last_spec = lines
        scratch = []
    return pl.pallas_call(
        functools.partial(head_kernel, pieces, steps, features, resumed, finished),
        grid=(steps,),
        in_specs=in_specs,
        out_specs=[whole, whole, last_spec],
        out_shape=[logits, logits, last],
        scratch_shapes=scratch,
        compiler_params=params(26),
        cost_estimate=pl.CostEstimate(
            flops=4 * rows * blocks * LINE * columns,
            bytes_accessed=4 * blocks * LINE * columns,
            transcendentals=0,
        ),
        name="expert_head",
    )(*gathered, own_weight, other_weight, gain, *(before or ()))


def amateur_kernel(place_ref, hidden_ref, weight_ref, logits_ref, stats_ref):
    logits = jnp.dot(
        hidden_ref[...], weight_ref[...], preferred_element_type=jnp.float32
    ).astype(jnp.bfloat16)
    logits_ref[...] = logits
    wide = logits.astype(jnp.float32)
    largest = jnp.max(wide, axis=1, keepdims=True)
    totals = jnp.sum(jnp.exp(wide - largest), axis=1, keepdims=True)
    for plane in range(2):
        picks = range(plane * 8, wide.shape[0], 16)
        stats_ref[0, plane] = laid_along_lanes(
            jnp.concatenate([largest[at : at + 8] for at in picks], axis=0),
            jnp.concatenate([totals[at : at + 8] for at in picks], axis=0),
        )


def amateur_logits(hidden, weight, place, columns):
    rows, width = hidden.shape
    tall = 2 * LINE
    return pl.pallas_call(
        amateur_kernel,
        grid_spec=pltpu.PrefetchScalarGridSpec(
            num_scalar_prefetch=1,
            grid=(rows // tall,),
            in_specs=[
                pl.BlockSpec((tall, width), lambda i, place: (i, 0)),
                pl.BlockSpec((width, columns), lambda i, place: (0, place[0])),
            ],
            out_specs=[
                pl.BlockSpec((tall, columns), lambda i, place: (i, 0)),
                pl.BlockSpec((1, 2, 2, LINE), lambda i, place: (i, 0, 0, 0)),
            ],
        ),
        out_shape=[
            pltpu.HBM((rows, columns), jnp.bfloat16),
            jax.ShapeDtypeStruct((rows // tall, 2, 2, LINE), jnp.float32),
        ],
        compiler_params=params(16),
        cost_estimate=pl.CostEstimate(
            flops=2 * rows * width * columns,
            bytes_accessed=2 * (rows * width + width * columns + rows * columns),
            transcendentals=rows * columns,
        ),
        name="amateur_head",
    )(place, hidden, weight)


def merged(parts):
    largest = jnp.max(parts[:, :, 0], axis=0)
    totals = jnp.sum(parts[:, :, 1] * jnp.exp(parts[:, :, 0] - largest[None]), axis=0)
    return largest, totals


def spread_kernel(
    place_ref, first_ref, rest_ref, amateur_ref, out_ref, stats_ref, group_ref, sem
):
    quarters = amateur_ref.shape[0] // 2
    for piece in range(quarters):
        at = pl.ds(2 * lax.rem(place_ref[0] + piece, quarters), 2)
        stats_ref[at] = first_ref[...] if piece == 0 else rest_ref[2 * piece - 2 : 2 * piece]
    amateur = amateur_ref[...]
    rows = []
    for quarter in range(quarters):
        at = 2 * quarter
        largest = stats_ref[at : at + 1]
        coarse = largest.astype(jnp.bfloat16).astype(jnp.float32)
        amateur_lse = amateur[at : at + 1] + jnp.log(amateur[at + 1 : at + 2])
        rows += [
            coarse,
            largest - coarse,
            stats_ref[at + 1 : at + 2],
            amateur_lse - largest,
        ]
    packed = jnp.concatenate(rows, axis=0).astype(jnp.bfloat16)
    many = group_ref.shape[0]
    for target in range(many):
        group_ref[target] = packed
    copies = [
        pltpu.make_async_copy(group_ref, out_ref.at[pl.ds(at, many)], sem.at[at // many])
        for at in range(0, out_ref.shape[0], many)
    ]
    for copy in copies:
        copy.start()
    for copy in copies:
        copy.wait()


def spread(place, first, rest, amateur, targets):
    rows = 2 * amateur.shape[0]
    many = 16
    vmem = pl.BlockSpec(memory_space=pltpu.VMEM)
    return pl.pallas_call(
        spread_kernel,
        in_specs=[pl.BlockSpec(memory_space=pltpu.SMEM)] + [vmem] * 3,
        out_specs=pl.BlockSpec(memory_space=pltpu.HBM),
        out_shape=pltpu.HBM((targets, rows, LINE), jnp.bfloat16),
        scratch_shapes=[
            pltpu.VMEM(amateur.shape, jnp.float32),
            pltpu.VMEM((many, rows, LINE), jnp.bfloat16),
            pltpu.SemaphoreType.DMA((targets // many,)),
        ],
        compiler_params=params(4),
        name="spread_stats",
    )(place, first, rest, amateur)


def merge_kernel(parts_ref, out_ref):
    parts = parts_ref[...].astype(jnp.float32)
    tops, shifts = [], []
    for quarter in range(out_ref.shape[0] // 2):
        coarse, fine, sums, apart = (parts[:, 4 * quarter + i] for i in range(4))
        largest = coarse + fine
        amateur = largest + apart
        top = jnp.max(largest, axis=0, keepdims=True)
        amateur_top = jnp.max(amateur, axis=0, keepdims=True)
        total = jnp.sum(sums * jnp.exp(largest - top), axis=0, keepdims=True)
        amateur_total = jnp.sum(jnp.exp(amateur - amateur_top), axis=0, keepdims=True)
        tops.append(top)
        shifts.append((top + jnp.log(total)) - (amateur_top + jnp.log(amateur_total)))
    out_ref[...] = jnp.concatenate(tops + shifts, axis=0)


def merge(parts):
    return pl.pallas_call(
        merge_kernel,
        out_shape=jax.ShapeDtypeStruct((parts.shape[1] // 2, LINE), jnp.float32),
        compiler_params=params(8),
        name="merge_stats",
    )(parts)


def column_of(row):
    return jnp.transpose(jnp.broadcast_to(row, (LINE, LINE)))


def contrast_kernel(
    place_ref,
    mine_ref,
    theirs_ref,
    limit_ref,
    own_first_in,
    own_rest_in,
    other_first_in,
    other_rest_in,
    amateur_in,
    out_ref,
    own_first,
    own_rest,
    other_first,
    other_rest,
    amateur_ref,
    result_ref,
    sem,
    sem_in,
):
    quarters = limit_ref.shape[0] // 2
    tall = 2 * LINE

    def arrivals(piece):
        at = pl.ds(max(piece - 1, 0) * LINE, LINE)
        sides = (
            ((own_first_in, own_first), (other_first_in, other_first))
            if piece == 0
            else ((own_rest_in, own_rest), (other_rest_in, other_rest))
        )
        quarter = lax.rem(place_ref[0] + piece, quarters)
        rows = pl.ds(pl.multiple_of(quarter * tall, tall), tall)
        pairs = [(source.at[at], target.at[at]) for source, target in sides]
        pairs.append((amateur_in.at[rows], amateur_ref.at[rows]))
        return [
            pltpu.make_async_copy(source, target, sem_in.at[piece, i])
            for i, (source, target) in enumerate(pairs)
        ]

    ahead = 2
    for piece in range(ahead):
        for copy in arrivals(piece):
            copy.start()
    core = place_ref[1]
    first = core == 0
    step_rows = 32
    copies = []
    for piece in range(quarters):
        quarter = lax.rem(place_ref[0] + piece, quarters)
        start = pl.multiple_of(quarter * tall, tall)
        sides = []
        for stats, plane in ((mine_ref, core), (theirs_ref, 1 - core)):
            top = stats[pl.ds(quarter, 1)]
            limit = limit_ref[pl.ds(plane * quarters + quarter, 1)]
            sides.append(
                (column_of(limit - top), column_of(stats[pl.ds(quarters + quarter, 1)]))
            )
        for copy in arrivals(piece):
            copy.wait()
        if piece + ahead < quarters:
            for copy in arrivals(piece + ahead):
                copy.start()
        experts = (own_first, other_first) if piece == 0 else (own_rest, other_rest)
        offset = 0 if piece == 0 else (piece - 1) * LINE
        for at in range(0, LINE, step_rows):
            rows = slice(at, at + step_rows)
            own, other = (
                expert - shift[rows, :1] + jnp.minimum(expert + limit[rows, :1], 0.0)
                for expert, (limit, shift) in zip(
                    (ref[offset + at : offset + at + step_rows] for ref in experts), sides
                )
            )
            planes = (jnp.where(first, own, other), jnp.where(first, other, own))
            mixed = jnp.concatenate(
                [plane[i : i + 8] for i in range(0, step_rows, 8) for plane in planes], axis=0
            )
            amateur = amateur_ref[pl.ds(pl.multiple_of(start + 2 * at, 2 * step_rows), 2 * step_rows)]
            result_ref[piece, 2 * at : 2 * at + 2 * step_rows] = mixed - amateur.astype(jnp.float32)
        copy = pltpu.make_async_copy(
            result_ref.at[piece], out_ref.at[pl.ds(start, tall)], sem.at[piece]
        )
        copy.start()
        copies.append(copy)
    for copy in copies:
        copy.wait()


def contrast(place, mine, theirs, limit, own, other, amateur):
    rows, columns = amateur.shape
    vmem = pl.BlockSpec(memory_space=pltpu.VMEM)
    return pl.pallas_call(
        contrast_kernel,
        in_specs=[pl.BlockSpec(memory_space=pltpu.SMEM)]
        + [vmem] * 3
        + [pl.BlockSpec(memory_space=pl.ANY)] * 5,
        out_specs=pl.BlockSpec(memory_space=pl.ANY),
        out_shape=jax.ShapeDtypeStruct((rows, columns), jnp.float32),
        scratch_shapes=[pltpu.VMEM(a.shape, a.dtype) for a in (*own, *other, amateur)]
        + [
            pltpu.VMEM((rows // (2 * LINE), 2 * LINE, columns), jnp.float32),
            pltpu.SemaphoreType.DMA((rows // (2 * LINE),)),
            pltpu.SemaphoreType.DMA((4, 3)),
        ],
        compiler_params=params(60),
        cost_estimate=pl.CostEstimate(
            flops=6 * rows * columns, bytes_accessed=10 * rows * columns, transcendentals=0
        ),
        name="contrast",
    )(place, mine, theirs, limit, own[0], own[1], other[0], other[1], amateur)


def body(
    queries,
    cache_keys,
    cache_values,
    new_keys,
    new_values,
    lengths,
    residual,
    gain,
    out_weight,
    head_weight,
    amateur_hidden,
    amateur_head,
    thresholds,
):
    z, y, x = (lax.axis_index(axis) for axis in CHIPS)
    core = lax.axis_index("core")
    first = core == 0
    sizes = tuple(lax.axis_size(axis) for axis in CHIPS)
    depth, chips = sizes[0], int(np.prod(sizes))
    per, width = queries.shape
    rows = residual.shape[0]
    columns = head_weight.shape[1]
    slab = width // depth
    heads = QH // depth
    quarter = quarter_of(z, y, x)

    attention = attend(queries, cache_keys, cache_values, new_keys, new_values, lengths)
    slabs = attention.reshape(per, depth, heads, LINE).transpose(1, 2, 0, 3)
    copies = copied(slabs.reshape(depth, heads * per, LINE), chips // depth)
    copies = copies.reshape(chips * heads * per, LINE)
    copies, residual, kept_weight = lax.optimization_barrier((copies, residual, out_weight))
    everyone = lax.all_gather(amateur_hidden, "z", axis=0, tiled=True)
    arrived = lax.all_to_all(copies, CHIPS, split_axis=0, concat_axis=0, tiled=True)

    other_weight = shift(head_weight, "core", 1)

    pieces = []
    for step in range(depth):
        turned = (kept_weight if step == 0 else out_weight).T
        part = lax.dynamic_slice_in_dim(turned, lax.rem(z + step, depth) * slab, slab, 1)
        pieces.append(part if step == 0 else shift(part, "z", step))
    mine = jnp.stack(pieces)
    theirs = shift(mine, "core", 1)
    projection = jnp.stack(
        [jnp.where(first, mine, theirs), jnp.where(first, theirs, mine)], axis=1
    ).reshape(depth * 2 * turned.shape[0], slab)

    planes = residual.T.reshape(-1, chips, 2, per)
    kept = lax.dynamic_index_in_dim(planes, core, 2, False)
    given = shift(lax.dynamic_index_in_dim(planes, 1 - core, 2, False), "core", 1)
    base = jnp.concatenate([jnp.where(first, kept, given), jnp.where(first, given, kept)], axis=0)
    base = base.reshape(-1, chips * per).T

    left = arrived.reshape(chips, heads, per, LINE).transpose(0, 2, 1, 3).reshape(chips * per, slab)
    projection = pltpu.with_memory_space_constraint(projection, pltpu.HBM)
    total, *sent = project(left, projection, base)
    parts = [shift(part, "z", -step) for step, part in enumerate(sent, 1)]
    total, everyone = lax.optimization_barrier((total, everyone))

    turns = [quarter_of(*place, 0) for place in np.ndindex(*sizes[:2])]
    copies = hidden_copies(total, parts, turns).reshape(chips, LINE, LINE)
    quarters = lax.all_to_all(copies, CHIPS, split_axis=0, concat_axis=0, tiled=True)
    amateur, amateur_stats = amateur_logits(everyone, amateur_head, z.reshape(1), columns)
    by_plane = amateur_stats.transpose(1, 0, 2, 3)
    kept = lax.dynamic_index_in_dim(by_plane, core, 0, False)
    given = shift(lax.dynamic_index_in_dim(by_plane, 1 - core, 0, False), "core", 1)
    amateur_chip = jnp.stack(merged(jnp.stack([kept, given])), axis=1)

    limit = thresholds.astype(jnp.float32).reshape(chips, 2, per).transpose(1, 0, 2)
    limit = limit.reshape(rows // LINE, LINE) * LOG_TWO
    place = jnp.stack([quarter, core])
    quarters, amateur, amateur_chip, limit, place = lax.optimization_barrier(
        (quarters, amateur, amateur_chip, limit, place)
    )
    moves = (
        ((0, 0, -1), (-1, 0, 0)),
        ((0, -1, 0), (0, 1, 0)),
        ((0, 0, 1), (1, 0, 0)),
    )
    half = chips * 6 // 8

    gain_lines = gain.reshape(-1, LINE)
    halves = [[shift_chips(quarters[:half], move) for move in moves]]
    halves.append([shift_chips(quarters[half:], move) for move in moves[:2]])
    far = [pltpu.with_memory_space_constraint(w, pltpu.HBM) for w in (head_weight, other_weight)]
    own_0, other_0, stats_0 = head([quarters], *far, gain_lines)
    later, own_0 = lax.optimization_barrier((quarters[half:], own_0))
    halves[1].append(shift_chips(later, moves[2]))
    begun = head(halves[0], head_weight, other_weight, gain_lines, finished=False)
    own_1, other_1, stats_1 = head(
        halves[1], head_weight, other_weight, gain_lines, start=half, before=begun
    )
    crossed = [shift(logits, "core", 1) for logits in (other_0, other_1)]

    copies = spread(place, stats_0, stats_1, amateur_chip.reshape(-1, LINE), chips)
    mine = merge(lax.all_to_all(copies, CHIPS, split_axis=0, concat_axis=0, tiled=True))
    theirs = shift(mine, "core", 1)
    return contrast(place, mine, theirs, limit, (own_0, own_1), crossed, amateur)


def solution(mesh):
    fine = Mesh(mesh.devices.reshape(4, 4, 4, 2), ALL)
    every = ALL
    by_vocab = ("y", "x", "core")
    in_specs = (
        P(every, None),
        P(every, None, None),
        P(every, None, None),
        P(every, None),
        P(every, None),
        P(every),
        P(None, every),
        P(),
        P(None, every),
        P(None, by_vocab + ("z",)),
        P("z", None),
        P(None, by_vocab),
        P(),
    )
    out_specs = P(None, by_vocab + ("z",))
    return jax.shard_map(body, mesh=fine, in_specs=in_specs, out_specs=out_specs, check_vma=False)
```
